512 devices in a mesh: row: 32 (over y, x), col: 16 (over z, core).
Axes of the slice: x: 4, y: 8, z: 8, core: 2. Of those that a mesh axis runs over, the one named last changes fastest.
Arguments:
- features: bfloat16 [65536, 512], P(('col', 'row')), may hold values from -6 to 6
- weight: bfloat16 [512, 512], replicated, may hold values from -0.25 to 0.25
- cotangent: bfloat16 [65536, 512], P(('row', 'col')), may hold values from -6 to 6
- tile_values: bfloat16 [32, 16, 8, 128, 128], P('row', 'col'), may hold values from -0.1875 to 0.1875
- tile_rows: int32 [32, 16, 8], P('row', 'col'), may hold values from 0 to 15
- tile_cols: int32 [32, 16, 8], P('row', 'col'), may hold values from 0 to 31
- tile_valid: int32 [32, 16, 8], P('row', 'col'), may hold values from 0 to 1, as said below
Outputs:
- activations: bfloat16 [65536, 512], P(('row', 'col'))
- input_grad: bfloat16 [65536, 512], P(('col', 'row'))
- weight_grad: float32 [512, 512], replicated
The draws below stay inside these ranges and needn't reach their ends.
Inputs may be any that keep to these rules, and one draw needn't show every extreme that they name: `tile_valid`: in each grid block the valid slots come first; every block has at least one, and some block has all 8.
All inputs are finite; a program needn't handle non-finite values.
Results may differ from the reference program's by a relative error of at most 0.02.
Values may be sent and summed in bfloat16 or wider, within the bound.
No kernel may reach another device: no remote copies, remote signals or barrier semaphores. Data moves between devices by JAX's collectives and lax.ppermute only.
A program may use at most 64 MiB of HBM per device.

```python
import math
import jax
import jax.numpy as jnp
from jax import lax

F = 512
TILE = 128
SLOTS = 8
GRID_ROWS = 32
GRID_COLS = 16
NODES = 65536
ROW_TILES = 16
COL_TILES = 32
N_COL = 16


def draw_tile_valid(key, part):
    key = jax.random.fold_in(key, 11)
    count_key, pick_key = jax.random.split(key)
    counts = jax.random.randint(count_key, (GRID_ROWS * GRID_COLS,), 1, SLOTS + 1)
    chosen = jax.random.randint(pick_key, (), 0, GRID_ROWS * GRID_COLS)
    counts = jnp.where(jnp.arange(GRID_ROWS * GRID_COLS) == chosen, SLOTS, counts)
    counts = counts.reshape(GRID_ROWS, GRID_COLS)
    slot_ids = jnp.arange(SLOTS, dtype=jnp.int32)
    return (slot_ids[None, None, :] < counts[:, :, None]).astype(jnp.int32)


def with_ends(drawn, stream_key, least, largest):
    index_at = [jax.random.randint(jax.random.fold_in(stream_key, axis), (), 0, length) for axis, length in enumerate(drawn.shape)]
    widest = drawn.shape.index(max(drawn.shape))
    neighbour = index_at[:widest] + [(index_at[widest] + 1) % drawn.shape[widest]] + index_at[widest + 1:]
    return drawn.at[tuple(index_at)].set(least).at[tuple(neighbour)].set(largest)


def shard_levels(stream_key, extent, cuts, low, top_value):
    factor_of, own = 1.0, jax.random.fold_in(stream_key, 6)
    for dim, shards_of in cuts:
        draws = jnp.exp(jax.random.uniform(jax.random.fold_in(own, dim), (shards_of,), jnp.float32, low / len(cuts), top_value / len(cuts)))
        factor_of = factor_of * jnp.repeat(draws, extent[dim] // shards_of).reshape([-1 if axis == dim else 1 for axis in range(len(extent))])
    return factor_of


def scatter_about(own_key, extent, scale, bound, cuts=(), kind=jnp.bfloat16):
    array = scale * jax.random.normal(own_key, extent, jnp.float32)
    if cuts:
        array = array * shard_levels(own_key, extent, cuts, -0.22, 0.18)
    return jnp.clip(array, -bound, bound).astype(kind)


def setup_inputs(seed: int = 0) -> dict:
    seeds = jax.random.split(jax.random.key(seed), 8)
    return {
        "features": scatter_about(seeds[0], (NODES, F), 1.0, 6.0, ((0, 512),)),
        "weight": scatter_about(seeds[1], (F, F), F ** -0.5, 0.25),
        "cotangent": scatter_about(seeds[2], (NODES, F), 1.0, 6.0, ((0, 512),)),
        "tile_values": scatter_about(seeds[3], (GRID_ROWS, GRID_COLS, SLOTS, TILE, TILE), (TILE * SLOTS * N_COL // ROW_TILES) ** -0.5, 0.1875, ((0, 32), (1, 16))),
        "tile_rows": with_ends(jax.random.randint(seeds[4], (GRID_ROWS, GRID_COLS, SLOTS), 0, ROW_TILES), jax.random.fold_in(seeds[4], 1), 0, ROW_TILES - 1).astype(jnp.int32),
        "tile_cols": with_ends(jax.random.randint(seeds[5], (GRID_ROWS, GRID_COLS, SLOTS), 0, COL_TILES), jax.random.fold_in(seeds[5], 1), 0, COL_TILES - 1).astype(jnp.int32),
        "tile_valid": draw_tile_valid(jax.random.fold_in(seeds[7], 71), 0),
    }


def tile_block(values, out_index, in_index, valid_flags, panel, out_count, transposed):
    tile_size = values.shape[-1]
    width = panel.shape[-1]
    pieces = panel.reshape(-1, tile_size, width)[in_index.astype(jnp.int32)]
    form = 'sji,sjf->sif' if transposed else 'sij,sjf->sif'
    products = jnp.einsum(form, values.astype(jnp.float32), pieces.astype(jnp.float32))
    selector = ((out_index[None, :] == jnp.arange(out_count, dtype=jnp.int32)[:, None]) & (valid_flags[None, :] > 0)).astype(jnp.float32)
    summed = jnp.einsum('rs,sif->rif', selector, products, precision=lax.Precision.HIGHEST)
    return summed.reshape(out_count * tile_size, width)

def reference(features, weight, cotangent, tile_values, tile_rows, tile_cols, tile_valid):
    width = weight.shape[0]
    grid_rows = tile_values.shape[0]
    grid_cols = tile_values.shape[1]
    row_block = NODES // grid_rows
    col_block = NODES // grid_cols
    projected = jnp.dot(features, weight, preferred_element_type=jnp.float32).astype(jnp.bfloat16)

    def forward_row(row_id):

        def add_block(total, col_id):
            panel = lax.dynamic_slice_in_dim(projected, col_id * col_block, col_block, 0)
            term = tile_block(tile_values[row_id, col_id], tile_rows[row_id, col_id], tile_cols[row_id, col_id], tile_valid[row_id, col_id], panel, ROW_TILES, False)
            return (total + term.astype(jnp.bfloat16).astype(jnp.float32), None)
        total, unused = lax.scan(add_block, jnp.zeros((row_block, width), jnp.float32), jnp.arange(grid_cols, dtype=jnp.int32))
        return total
    aggregated = lax.map(forward_row, jnp.arange(grid_rows, dtype=jnp.int32)).reshape(NODES, width)
    activations = jax.nn.silu(aggregated).astype(jnp.bfloat16)
    sig = jax.nn.sigmoid(aggregated)
    grad_pre = (cotangent.astype(jnp.float32) * sig * (1.0 + aggregated * (1.0 - sig))).astype(jnp.bfloat16)

    def backward_col(col_id):

        def add_block(total, row_id):
            panel = lax.dynamic_slice_in_dim(grad_pre, row_id * row_block, row_block, 0)
            term = tile_block(tile_values[row_id, col_id], tile_cols[row_id, col_id], tile_rows[row_id, col_id], tile_valid[row_id, col_id], panel, COL_TILES, True)
            return (total + term.astype(jnp.bfloat16).astype(jnp.float32), None)
        total, unused = lax.scan(add_block, jnp.zeros((col_block, width), jnp.float32), jnp.arange(grid_rows, dtype=jnp.int32))
        return total
    grad_projected = lax.map(backward_col, jnp.arange(grid_cols, dtype=jnp.int32)).reshape(NODES, width).astype(jnp.bfloat16)
    input_grad = jnp.dot(grad_projected, weight.T, preferred_element_type=jnp.float32).astype(jnp.bfloat16)
    weight_grad = jnp.dot(features.T, grad_projected, preferred_element_type=jnp.float32) * (1.0 / math.sqrt(NODES))
    return (activations, input_grad, weight_grad)
```

```python
import math

import jax
import jax.numpy as jnp
from jax import lax
from jax.experimental import pallas as pl
from jax.experimental.pallas import tpu as pltpu
from jax.sharding import Mesh, PartitionSpec as P

Y, X, Z, CORES = 8, 4, 8, 2
TILE = 128
SLOTS = 8
WIDTH = 512
CHUNK = WIDTH // X
ROW_TILES = Z * CORES
COL_TILES = Y * X
INDEX_ROWS = 16
BF16 = jnp.bfloat16
F32 = jnp.float32


def params():
    return pltpu.CompilerParams(vmem_limit_bytes=24 * 1024 * 1024)


def vmem():
    return pl.BlockSpec(memory_space=pltpu.VMEM)


def smem():
    return pl.BlockSpec(memory_space=pltpu.SMEM)


def forward_tiles(core_ref, index_ref, tiles_ref, panel_ref, mine_ref, other_ref, total):
    block = pl.program_id(0)
    core = core_ref[0]
    total[...] = jnp.zeros_like(total)
    for slot in range(SLOTS):
        row = index_ref[block, slot]
        col = index_ref[block, SLOTS + slot]
        valid = index_ref[block, 2 * SLOTS + slot]
        product = jnp.dot(
            tiles_ref[0, slot * TILE : (slot + 1) * TILE, :], panel_ref[col], preferred_element_type=F32
        )
        total[row] += jnp.where(valid > 0, product, 0.0)
    for pair in range(Z):
        mine_ref[0, pair] = total[2 * pair + core].astype(BF16)
        other_ref[0, pair] = total[2 * pair + 1 - core].astype(BF16)


def middle(parts_ref, weight_ref, cotangent_ref, act_ref, grad_ref, weight_part_ref):
    chunks = []
    for chunk in range(X):
        total = parts_ref[chunk * Z].astype(F32)
        for z in range(1, Z):
            total += parts_ref[chunk * Z + z].astype(F32)
        chunks.append(total)
    summed = jnp.concatenate(chunks, axis=1)
    high = summed.astype(BF16)
    low = (summed - high.astype(F32)).astype(BF16)
    weight = weight_ref[...]
    aggregated = jnp.dot(high, weight, preferred_element_type=F32) + jnp.dot(
        low, weight, preferred_element_type=F32
    )
    sig = jax.nn.sigmoid(aggregated)
    act_ref[...] = (aggregated * sig).astype(BF16)
    grad = (cotangent_ref[...].astype(F32) * sig * (1.0 + aggregated * (1.0 - sig))).astype(BF16)
    for chunk in range(X):
        piece = grad[:, chunk * CHUNK : (chunk + 1) * CHUNK]
        for z in range(Z):
            grad_ref[chunk * Z + z] = piece
    weight_part_ref[...] = lax.dot_general(
        high, grad, (((0,), (0,)), ((), ())), preferred_element_type=F32
    ).astype(BF16)


def backward_tiles(core_ref, index_ref, tiles_ref, mine_ref, other_ref, out_ref, total):
    core = core_ref[0]
    total[...] = jnp.zeros_like(total)
    for block in range(X):
        for slot in range(SLOTS):
            row = index_ref[block, slot]
            col = index_ref[block, SLOTS + slot]
            valid = index_ref[block, 2 * SLOTS + slot]
            at = block * Z + row // 2
            panel = jnp.where(row % 2 == core, mine_ref[at], other_ref[at])
            product = lax.dot_general(
                tiles_ref[block, slot * TILE : (slot + 1) * TILE, :],
                panel,
                (((0,), (0,)), ((), ())),
                preferred_element_type=F32,
            )
            total[col] += jnp.where(valid > 0, product, 0.0)
    for tile in range(COL_TILES):
        out_ref[tile] = total[tile].astype(BF16)


def last(parts_ref, weight_ref, out_ref):
    chunks = []
    for chunk in range(X):
        total = parts_ref[chunk].astype(F32)
        for y in range(1, Y):
            total += parts_ref[y * X + chunk].astype(F32)
        chunks.append(total)
    summed = jnp.concatenate(chunks, axis=1).astype(BF16)
    out_ref[...] = lax.dot_general(
        summed, weight_ref[...], (((1,), (1,)), ((), ())), preferred_element_type=F32
    ).astype(BF16)


def body(features, weight, cotangent, tile_values, tile_rows, tile_cols, tile_valid):
    core = lax.axis_index("core").astype(jnp.int32)[None]

    index = jnp.concatenate(
        [tile_rows.reshape(-1), tile_cols.reshape(-1), tile_valid.reshape(-1)]
    ).astype(BF16)
    index = jnp.pad(index[None, :], ((0, INDEX_ROWS - 1), (0, TILE - 3 * SLOTS)))
    tiles = jnp.concatenate([tile_values.reshape(SLOTS * TILE, TILE), index], axis=0)
    tiles = lax.all_gather(tiles, "x", axis=0)
    index = tiles[:, SLOTS * TILE, : 3 * SLOTS].astype(jnp.int32)
    limit = jnp.repeat(jnp.array([ROW_TILES - 1, COL_TILES - 1, 1], jnp.int32), SLOTS)
    index = jnp.clip(index, 0, limit[None, :])

    chunks = features.reshape(TILE, X, CHUNK).transpose(1, 0, 2)
    chunks = jnp.broadcast_to(chunks[None], (Y, X, TILE, CHUNK)).reshape(COL_TILES, TILE, CHUNK)
    panel = lax.all_to_all(chunks, ("y", "x"), 0, 0, tiled=True)

    rows = SLOTS * TILE + INDEX_ROWS
    mine, other = pl.pallas_call(
        forward_tiles,
        grid=(X,),
        in_specs=[
            smem(),
            smem(),
            pl.BlockSpec((1, rows, TILE), lambda i: (i, 0, 0)),
            pl.BlockSpec((COL_TILES, TILE, CHUNK), lambda i: (0, 0, 0)),
        ],
        out_specs=[pl.BlockSpec((1, Z, TILE, CHUNK), lambda i: (i, 0, 0, 0))] * 2,
        out_shape=[jax.ShapeDtypeStruct((X, Z, TILE, CHUNK), BF16)] * 2,
        scratch_shapes=[pltpu.VMEM((ROW_TILES, TILE, CHUNK), F32)],
        compiler_params=params(),
        name="forward_tiles",
    )(core, index, tiles, panel)

    swap = [(0, 1), (1, 0)]
    term = (mine.astype(F32) + lax.ppermute(other, "core", swap).astype(F32)).astype(BF16)
    parts = lax.all_to_all(term.reshape(X * Z, TILE, CHUNK), ("x", "z"), 0, 0, tiled=True)

    activations, grad, weight_part = pl.pallas_call(
        middle,
        in_specs=[vmem()] * 3,
        out_specs=[vmem()] * 3,
        out_shape=[
            jax.ShapeDtypeStruct((TILE, WIDTH), BF16),
            jax.ShapeDtypeStruct((X * Z, TILE, CHUNK), BF16),
            jax.ShapeDtypeStruct((WIDTH, WIDTH), BF16),
        ],
        compiler_params=params(),
        name="middle",
    )(parts, weight, cotangent)

    grad_mine = lax.all_to_all(grad, ("x", "z"), 0, 0, tiled=True)
    grad_other = lax.ppermute(grad_mine, "core", swap)

    group = Y * X * CORES
    share = WIDTH // group
    pieces = lax.all_to_all(
        weight_part.reshape(group, share, WIDTH), ("y", "x", "core"), 0, 0, tiled=True
    )
    piece = pieces.astype(F32).sum(0).astype(BF16)
    piece = lax.all_to_all(
        jnp.broadcast_to(piece[None], (Z, share, WIDTH)), "z", 0, 0, tiled=True
    )
    piece = piece.astype(F32).sum(0).astype(BF16)
    whole = lax.all_to_all(
        jnp.broadcast_to(piece[None], (group, share, WIDTH)), ("y", "x", "core"), 0, 0, tiled=True
    )
    nodes = TILE * Y * X * Z * CORES
    weight_grad = whole.reshape(WIDTH, WIDTH).astype(F32) * (1.0 / math.sqrt(nodes))

    back = pl.pallas_call(
        backward_tiles,
        in_specs=[smem(), smem(), vmem(), vmem(), vmem()],
        out_specs=vmem(),
        out_shape=jax.ShapeDtypeStruct((COL_TILES, TILE, CHUNK), BF16),
        scratch_shapes=[pltpu.VMEM((COL_TILES, TILE, CHUNK), F32)],
        compiler_params=params(),
        name="backward_tiles",
    )(core, index, tiles, grad_mine, grad_other)
    back = lax.all_to_all(back, ("y", "x"), 0, 0, tiled=True)

    input_grad = pl.pallas_call(
        last,
        in_specs=[vmem()] * 2,
        out_specs=vmem(),
        out_shape=jax.ShapeDtypeStruct((TILE, WIDTH), BF16),
        compiler_params=params(),
        name="last",
    )(back, weight)
    return (activations, input_grad, weight_grad)


def solution(mesh):
    axes = Mesh(mesh.devices.reshape(Y, X, Z, CORES), ("y", "x", "z", "core"))
    row, col = ("y", "x"), ("z", "core")
    placed = (
        P(col + row, None),
        P(),
        P(row + col, None),
        P(row, col, None, None, None),
        P(row, col, None),
        P(row, col, None),
        P(row, col, None),
    )
    return jax.shard_map(
        body,
        mesh=axes,
        in_specs=placed,
        out_specs=(P(row + col, None), P(col + row, None), P()),
        check_vma=False,
    )
```

```python
import math

import jax
import jax.numpy as jnp
from jax import lax
from jax.experimental import pallas as pl
from jax.experimental.pallas import tpu as pltpu
from jax.sharding import Mesh, PartitionSpec as P

Y, X, Z, CORES = 8, 4, 8, 2
TILE = 128
SLOTS = 8
WIDTH = 512
CHUNK = WIDTH // X
ROW_TILES = Z * CORES
COL_TILES = Y * X
INDEX_ROWS = 16
BF16 = jnp.bfloat16
F32 = jnp.float32


def params():
    return pltpu.CompilerParams(vmem_limit_bytes=24 * 1024 * 1024)


def vmem():
    return pl.BlockSpec(memory_space=pltpu.VMEM)


def smem():
    return pl.BlockSpec(memory_space=pltpu.SMEM)


def spread(features_ref, out_ref):
    for chunk in range(X):
        piece = features_ref[:, chunk * CHUNK : (chunk + 1) * CHUNK]
        for y in range(Y):
            out_ref[y * X + chunk] = piece


def forward_tiles(place_ref, index_ref, panel_ref, *refs):
    tiles_refs, (mine_ref, other_ref, total) = refs[:X], refs[X:]
    core = place_ref[0]
    for step in range(X):
        block = place_ref[1] ^ step
        total[...] = jnp.zeros_like(total)
        for slot in range(SLOTS):
            row = index_ref[step, slot]
            col = index_ref[step, SLOTS + slot]
            valid = index_ref[step, 2 * SLOTS + slot]
            tile = tiles_refs[step][slot * TILE : (slot + 1) * TILE, :]
            product = jnp.dot(tile, panel_ref[col], preferred_element_type=F32)
            total[row] += jnp.where(valid > 0, product, 0.0)
        for pair in range(Z):
            mine_ref[block * Z + pair] = total[2 * pair + core].astype(BF16)
            other_ref[block * Z + pair] = total[2 * pair + 1 - core].astype(BF16)


def middle(core_ref, parts_ref, weight_ref, cotangent_ref, act_ref, grad_ref, keep_ref, send_ref):
    chunks = []
    for chunk in range(X):
        total = parts_ref[chunk * Z].astype(F32)
        for z in range(1, Z):
            total += parts_ref[chunk * Z + z].astype(F32)
        chunks.append(total)
    summed = jnp.concatenate(chunks, axis=1)
    high = summed.astype(BF16)
    low = (summed - high.astype(F32)).astype(BF16)
    weight = weight_ref[...]
    aggregated = jnp.dot(high, weight, preferred_element_type=F32) + jnp.dot(
        low, weight, preferred_element_type=F32
    )
    sig = jax.nn.sigmoid(aggregated)
    act_ref[...] = (aggregated * sig).astype(BF16)
    grad = (cotangent_ref[...].astype(F32) * sig * (1.0 + aggregated * (1.0 - sig))).astype(BF16)
    for chunk in range(X):
        piece = grad[:, chunk * CHUNK : (chunk + 1) * CHUNK]
        for z in range(Z):
            grad_ref[chunk * Z + z] = piece
    weight_part = lax.dot_general(
        high, grad, (((0,), (0,)), ((), ())), preferred_element_type=F32
    ).astype(BF16)
    low_half, high_half = weight_part[: WIDTH // 2], weight_part[WIDTH // 2 :]
    upper = core_ref[0] == 1
    keep_ref[...] = jnp.where(upper, high_half, low_half)
    send_ref[...] = jnp.where(upper, low_half, high_half)


def backward_tiles(place_ref, index_ref, mine_ref, other_ref, *refs):
    tiles_refs, (out_ref, total) = refs[:X], refs[X:]
    core = place_ref[0]
    total[...] = jnp.zeros_like(total)
    for step in range(X):
        block = place_ref[1] ^ step
        for slot in range(SLOTS):
            row = index_ref[step, slot]
            col = index_ref[step, SLOTS + slot]
            valid = index_ref[step, 2 * SLOTS + slot]
            at = block * Z + row // 2
            panel = jnp.where(row % 2 == core, mine_ref[at], other_ref[at])
            tile = tiles_refs[step][slot * TILE : (slot + 1) * TILE, :]
            product = lax.dot_general(
                tile, panel, (((0,), (0,)), ((), ())), preferred_element_type=F32
            )
            total[col] += jnp.where(valid > 0, product, 0.0)
    for tile in range(COL_TILES):
        out_ref[tile] = total[tile].astype(BF16)


def last(parts_ref, weight_ref, out_ref):
    chunks = []
    for chunk in range(X):
        total = parts_ref[chunk].astype(F32)
        for y in range(1, Y):
            total += parts_ref[y * X + chunk].astype(F32)
        chunks.append(total)
    summed = jnp.concatenate(chunks, axis=1).astype(BF16)
    out_ref[...] = lax.dot_general(
        summed, weight_ref[...], (((1,), (1,)), ((), ())), preferred_element_type=F32
    ).astype(BF16)


def exchange(array, axis, distance):
    size = lax.axis_size(axis)
    return lax.ppermute(array, axis, [(i, i ^ distance) for i in range(size)])


def halve(array, axis, distance):
    upper = jnp.minimum(lax.axis_index(axis) & distance, 1)
    halves = array.reshape(2, array.shape[0] // 2, array.shape[1])
    send = lax.dynamic_index_in_dim(halves, 1 - upper, 0, keepdims=False)
    keep = lax.dynamic_index_in_dim(halves, upper, 0, keepdims=False)
    return (keep.astype(F32) + exchange(send, axis, distance).astype(F32)).astype(BF16)


def body(features, weight, cotangent, tile_values, tile_rows, tile_cols, tile_valid):
    place = jnp.stack([lax.axis_index("core"), lax.axis_index("x")]).astype(jnp.int32)

    chunks = pl.pallas_call(
        spread,
        in_specs=[vmem()],
        out_specs=vmem(),
        out_shape=jax.ShapeDtypeStruct((COL_TILES, TILE, CHUNK), BF16),
        compiler_params=params(),
        name="spread",
    )(features)
    panel = lax.all_to_all(chunks, ("y", "x"), 0, 0, tiled=True)

    index = jnp.concatenate(
        [tile_rows.reshape(-1), tile_cols.reshape(-1), tile_valid.reshape(-1)]
    ).astype(BF16)
    index = jnp.pad(index[None, :], ((0, INDEX_ROWS - 1), (0, TILE - 3 * SLOTS)))
    tiles = jnp.concatenate([tile_values.reshape(SLOTS * TILE, TILE), index], axis=0)
    tiles = [tiles] + [exchange(tiles, "x", distance) for distance in range(1, X)]
    index = jnp.stack([t[SLOTS * TILE, : 3 * SLOTS] for t in tiles]).astype(jnp.int32)
    limit = jnp.repeat(jnp.array([ROW_TILES - 1, COL_TILES - 1, 1], jnp.int32), SLOTS)
    index = jnp.clip(index, 0, limit[None, :])

    mine, other = pl.pallas_call(
        forward_tiles,
        in_specs=[smem(), smem()] + [vmem()] * (1 + X),
        out_specs=[vmem()] * 2,
        out_shape=[jax.ShapeDtypeStruct((X * Z, TILE, CHUNK), BF16)] * 2,
        scratch_shapes=[pltpu.VMEM((ROW_TILES, TILE, CHUNK), F32)],
        compiler_params=params(),
        name="forward_tiles",
    )(place, index, panel, *tiles)
    term = (mine.astype(F32) + exchange(other, "core", 1).astype(F32)).astype(BF16)
    parts = lax.all_to_all(term, ("x", "z"), 0, 0, tiled=True)

    half = WIDTH // CORES
    activations, grad, weight_keep, weight_send = pl.pallas_call(
        middle,
        in_specs=[smem()] + [vmem()] * 3,
        out_specs=[vmem()] * 4,
        out_shape=[
            jax.ShapeDtypeStruct((TILE, WIDTH), BF16),
            jax.ShapeDtypeStruct((X * Z, TILE, CHUNK), BF16),
            jax.ShapeDtypeStruct((half, WIDTH), BF16),
            jax.ShapeDtypeStruct((half, WIDTH), BF16),
        ],
        compiler_params=params(),
        name="middle",
    )(place, parts, weight, cotangent)

    grad_mine = lax.all_to_all(grad, ("x", "z"), 0, 0, tiled=True)
    piece = weight_keep.astype(F32) + exchange(weight_send, "core", 1).astype(F32)
    piece = piece.astype(BF16)
    for distance in (1, 2, 4):
        piece = halve(piece, "y", distance)
    grad_mine, piece = lax.optimization_barrier((grad_mine, piece))

    grad_other = exchange(grad_mine, "core", 1)
    back = pl.pallas_call(
        backward_tiles,
        in_specs=[smem(), smem()] + [vmem()] * (2 + X),
        out_specs=vmem(),
        out_shape=jax.ShapeDtypeStruct((COL_TILES, TILE, CHUNK), BF16),
        scratch_shapes=[pltpu.VMEM((COL_TILES, TILE, CHUNK), F32)],
        compiler_params=params(),
        name="backward_tiles",
    )(place, index, grad_mine, grad_other, *tiles)
    back, piece = lax.optimization_barrier((back, piece.astype(F32)))
    back = lax.all_to_all(back, ("y", "x"), 0, 0, tiled=True)
    for axis, distance in (("z", 1), ("z", 2), ("z", 4), ("x", 1), ("x", 2)):
        piece = piece + exchange(piece, axis, distance)
    back, piece = lax.optimization_barrier((back, piece))

    input_grad = pl.pallas_call(
        last,
        in_specs=[vmem()] * 2,
        out_specs=vmem(),
        out_shape=jax.ShapeDtypeStruct((TILE, WIDTH), BF16),
        compiler_params=params(),
        name="last",
    )(back, weight)

    share = WIDTH // (Y * CORES)
    piece = jnp.broadcast_to(piece.astype(BF16)[None], (Y * CORES, share, WIDTH))
    whole = lax.all_to_all(piece, ("y", "core"), 0, 0, tiled=True)
    whole = whole.reshape(2, 2, 2, CORES, share, WIDTH).transpose(3, 2, 1, 0, 4, 5)
    nodes = TILE * Y * X * Z * CORES
    weight_grad = whole.reshape(WIDTH, WIDTH).astype(F32) * (1.0 / math.sqrt(nodes))
    return (activations, input_grad, weight_grad)


def solution(mesh):
    axes = Mesh(mesh.devices.reshape(Y, X, Z, CORES), ("y", "x", "z", "core"))
    row, col = ("y", "x"), ("z", "core")
    placed = (
        P(col + row, None),
        P(),
        P(row + col, None),
        P(row, col, None, None, None),
        P(row, col, None),
        P(row, col, None),
        P(row, col, None),
    )
    return jax.shard_map(
        body,
        mesh=axes,
        in_specs=placed,
        out_specs=(P(row + col, None), P(col + row, None), P()),
        check_vma=False,
    )
```

```python
import math

import jax
import jax.numpy as jnp
from jax import lax
from jax.experimental import pallas as pl
from jax.experimental.pallas import tpu as pltpu
from jax.sharding import Mesh, PartitionSpec as P

Y, X, Z, CORES = 8, 4, 8, 2
TILE = 128
SLOTS = 8
WIDTH = 512
CHUNK = WIDTH // X
ROW_TILES = Z * CORES
COL_TILES = Y * X
BF16 = jnp.bfloat16
F32 = jnp.float32


def params():
    return pltpu.CompilerParams(vmem_limit_bytes=24 * 1024 * 1024)


def vmem():
    return pl.BlockSpec(memory_space=pltpu.VMEM)


def smem():
    return pl.BlockSpec(memory_space=pltpu.SMEM)


def spread(features_ref, out_ref):
    for chunk in range(X):
        piece = features_ref[:, chunk * CHUNK : (chunk + 1) * CHUNK]
        for y in range(Y):
            out_ref[y * X + chunk] = piece


def forward_tiles(place_ref, index_ref, panel_ref, *refs):
    tiles_refs, (mine_ref, other_ref, total) = refs[:X], refs[X:]
    core = place_ref[0]
    for step in range(X):
        block = place_ref[1] ^ step
        total[...] = jnp.zeros_like(total)
        for slot in range(SLOTS):
            row = index_ref[step, slot]
            col = index_ref[step, SLOTS + slot]
            valid = index_ref[step, 2 * SLOTS + slot]
            tile = tiles_refs[step][slot * TILE : (slot + 1) * TILE, :]
            product = jnp.dot(tile, panel_ref[col], preferred_element_type=F32)
            total[row] += jnp.where(valid > 0, product, 0.0)
        for pair in range(Z):
            mine_ref[block * Z + pair] = total[2 * pair + core].astype(BF16)
            other_ref[block * Z + pair] = total[2 * pair + 1 - core].astype(BF16)


def middle(core_ref, parts_ref, weight_ref, cotangent_ref, act_ref, grad_ref, keep_ref, send_ref):
    chunks = []
    for chunk in range(X):
        total = parts_ref[chunk * Z].astype(F32)
        for z in range(1, Z):
            total += parts_ref[chunk * Z + z].astype(F32)
        chunks.append(total)
    summed = jnp.concatenate(chunks, axis=1)
    high = summed.astype(BF16)
    low = (summed - high.astype(F32)).astype(BF16)
    weight = weight_ref[...]
    aggregated = jnp.dot(high, weight, preferred_element_type=F32) + jnp.dot(
        low, weight, preferred_element_type=F32
    )
    sig = jax.nn.sigmoid(aggregated)
    act_ref[...] = (aggregated * sig).astype(BF16)
    grad = (cotangent_ref[...].astype(F32) * sig * (1.0 + aggregated * (1.0 - sig))).astype(BF16)
    for chunk in range(X):
        piece = grad[:, chunk * CHUNK : (chunk + 1) * CHUNK]
        for z in range(Z):
            grad_ref[chunk * Z + z] = piece
    weight_part = lax.dot_general(
        high, grad, (((0,), (0,)), ((), ())), preferred_element_type=F32
    ).astype(BF16)
    low_half, high_half = weight_part[: WIDTH // 2], weight_part[WIDTH // 2 :]
    upper = core_ref[0] == 1
    keep_ref[...] = jnp.where(upper, high_half, low_half)
    send_ref[...] = jnp.where(upper, low_half, high_half)


def backward_tiles(place_ref, index_ref, mine_ref, other_ref, *refs):
    tiles_refs, (out_ref, total) = refs[:X], refs[X:]
    core = place_ref[0]
    total[...] = jnp.zeros_like(total)
    for step in range(X):
        block = place_ref[1] ^ step
        for slot in range(SLOTS):
            row = index_ref[step, slot]
            col = index_ref[step, SLOTS + slot]
            valid = index_ref[step, 2 * SLOTS + slot]
            at = block * Z + row // 2
            panel = jnp.where(row % 2 == core, mine_ref[at], other_ref[at])
            tile = tiles_refs[step][slot * TILE : (slot + 1) * TILE, :]
            product = lax.dot_general(
                tile, panel, (((0,), (0,)), ((), ())), preferred_element_type=F32
            )
            total[col] += jnp.where(valid > 0, product, 0.0)
    for tile in range(COL_TILES):
        out_ref[tile] = total[tile].astype(BF16)


def last(parts_ref, weight_ref, out_ref):
    chunks = []
    for chunk in range(X):
        total = parts_ref[chunk].astype(F32)
        for y in range(1, Y):
            total += parts_ref[y * X + chunk].astype(F32)
        chunks.append(total)
    summed = jnp.concatenate(chunks, axis=1).astype(BF16)
    out_ref[...] = lax.dot_general(
        summed, weight_ref[...], (((1,), (1,)), ((), ())), preferred_element_type=F32
    ).astype(BF16)


def place_rows(place_ref, mine_ref, other_ref, out_ref):
    core = place_ref[0]
    half, share = WIDTH // CORES, WIDTH // (Y * CORES)
    scale = 1.0 / math.sqrt(TILE * Y * X * Z * CORES)
    for y in range(Y):
        at = (y & 1) * 4 * share + (y >> 1 & 1) * 2 * share + (y >> 2) * share
        for side, ref in ((core, mine_ref), (1 - core, other_ref)):
            start = pl.multiple_of(side * half + at, share)
            out_ref[pl.ds(start, share), :] = ref[y].astype(F32) * scale


def exchange(array, axis, distance):
    size = lax.axis_size(axis)
    return lax.ppermute(array, axis, [(i, i ^ distance) for i in range(size)])


def halve(array, axis, distance):
    upper = jnp.minimum(lax.axis_index(axis) & distance, 1)
    halves = array.reshape(2, array.shape[0] // 2, array.shape[1])
    send = lax.dynamic_index_in_dim(halves, 1 - upper, 0, keepdims=False)
    keep = lax.dynamic_index_in_dim(halves, upper, 0, keepdims=False)
    return (keep.astype(F32) + exchange(send, axis, distance).astype(F32)).astype(BF16)


def body(features, weight, cotangent, tile_values, tile_rows, tile_cols, tile_valid):
    place = jnp.stack([lax.axis_index("core"), lax.axis_index("x")]).astype(jnp.int32)

    chunks = pl.pallas_call(
        spread,
        in_specs=[vmem()],
        out_specs=vmem(),
        out_shape=jax.ShapeDtypeStruct((COL_TILES, TILE, CHUNK), BF16),
        compiler_params=params(),
        name="spread",
    )(features)
    panel = lax.all_to_all(chunks, ("y", "x"), 0, 0, tiled=True)

    tiles = tile_values.reshape(SLOTS * TILE, TILE)
    tiles = [tiles] + [exchange(tiles, "x", distance) for distance in range(1, X)]
    index = jnp.concatenate([tile_rows, tile_cols, tile_valid], axis=2).reshape(1, 3 * SLOTS)
    index = jnp.concatenate([index] + [exchange(index, "x", distance) for distance in range(1, X)])

    mine, other = pl.pallas_call(
        forward_tiles,
        in_specs=[smem(), smem()] + [vmem()] * (1 + X),
        out_specs=[vmem()] * 2,
        out_shape=[jax.ShapeDtypeStruct((X * Z, TILE, CHUNK), BF16)] * 2,
        scratch_shapes=[pltpu.VMEM((ROW_TILES, TILE, CHUNK), F32)],
        compiler_params=params(),
        name="forward_tiles",
    )(place, index, panel, *tiles)
    term = (mine.astype(F32) + exchange(other, "core", 1).astype(F32)).astype(BF16)
    parts = lax.all_to_all(term, ("x", "z"), 0, 0, tiled=True)

    half = WIDTH // CORES
    activations, grad, weight_keep, weight_send = pl.pallas_call(
        middle,
        in_specs=[smem()] + [vmem()] * 3,
        out_specs=[vmem()] * 4,
        out_shape=[
            jax.ShapeDtypeStruct((TILE, WIDTH), BF16),
            jax.ShapeDtypeStruct((X * Z, TILE, CHUNK), BF16),
            jax.ShapeDtypeStruct((half, WIDTH), BF16),
            jax.ShapeDtypeStruct((half, WIDTH), BF16),
        ],
        compiler_params=params(),
        name="middle",
    )(place, parts, weight, cotangent)

    grad_mine = lax.all_to_all(grad, ("x", "z"), 0, 0, tiled=True)
    piece = weight_keep.astype(F32) + exchange(weight_send, "core", 1).astype(F32)
    piece = piece.astype(BF16)
    for distance in (1, 2, 4):
        piece = halve(piece, "y", distance)
    grad_mine, piece = lax.optimization_barrier((grad_mine, piece))

    grad_other = exchange(grad_mine, "core", 1)
    piece = piece.astype(F32)
    piece = piece + exchange(piece, "z", 1)
    back = pl.pallas_call(
        backward_tiles,
        in_specs=[smem(), smem()] + [vmem()] * (2 + X),
        out_specs=vmem(),
        out_shape=jax.ShapeDtypeStruct((COL_TILES, TILE, CHUNK), BF16),
        scratch_shapes=[pltpu.VMEM((COL_TILES, TILE, CHUNK), F32)],
        compiler_params=params(),
        name="backward_tiles",
    )(place, index, grad_mine, grad_other, *tiles)
    back, piece = lax.optimization_barrier((back, piece))
    back = lax.all_to_all(back, ("y", "x"), 0, 0, tiled=True)
    for axis, distance in (("z", 2), ("z", 4), ("x", 1), ("x", 2)):
        piece = piece + exchange(piece, axis, distance)
    back, piece = lax.optimization_barrier((back, piece))

    input_grad = pl.pallas_call(
        last,
        in_specs=[vmem()] * 2,
        out_specs=vmem(),
        out_shape=jax.ShapeDtypeStruct((TILE, WIDTH), BF16),
        compiler_params=params(),
        name="last",
    )(back, weight)

    share = WIDTH // (Y * CORES)
    piece = jnp.broadcast_to(piece.astype(BF16)[None], (Y, share, WIDTH))
    whole = lax.all_to_all(piece, "y", 0, 0, tiled=True)
    weight_grad = pl.pallas_call(
        place_rows,
        in_specs=[smem()] + [vmem()] * 2,
        out_specs=vmem(),
        out_shape=jax.ShapeDtypeStruct((WIDTH, WIDTH), F32),
        compiler_params=params(),
        name="place_rows",
    )(place, whole, exchange(whole, "core", 1))
    return (activations, input_grad, weight_grad)


def solution(mesh):
    axes = Mesh(mesh.devices.reshape(Y, X, Z, CORES), ("y", "x", "z", "core"))
    row, col = ("y", "x"), ("z", "core")
    placed = (
        P(col + row, None),
        P(),
        P(row + col, None),
        P(row, col, None, None, None),
        P(row, col, None),
        P(row, col, None),
        P(row, col, None),
    )
    return jax.shard_map(
        body,
        mesh=axes,
        in_specs=placed,
        out_specs=(P(row + col, None), P(col + row, None), P()),
        check_vma=False,
    )
```

```python
import math

import jax
import jax.numpy as jnp
from jax import lax
from jax.experimental import pallas as pl
from jax.experimental.pallas import tpu as pltpu
from jax.sharding import Mesh, PartitionSpec as P

Y, X, Z, CORES = 8, 4, 8, 2
TILE = 128
SLOTS = 8
WIDTH = 512
CHUNK = WIDTH // X
ROW_TILES = Z * CORES
COL_TILES = Y * X
BF16 = jnp.bfloat16
F32 = jnp.float32


def params():
    return pltpu.CompilerParams(vmem_limit_bytes=24 * 1024 * 1024)


def vmem():
    return pl.BlockSpec(memory_space=pltpu.VMEM)


def smem():
    return pl.BlockSpec(memory_space=pltpu.SMEM)


def spread(features_ref, out_ref):
    for chunk in range(X):
        piece = features_ref[:, chunk * CHUNK : (chunk + 1) * CHUNK]
        for y in range(Y):
            out_ref[y * X + chunk] = piece


def forward_tiles(place_ref, index_ref, panel_ref, *refs):
    tiles_refs, (mine_ref, other_ref, total) = refs[:X], refs[X:]
    core = place_ref[0]
    for step in range(X):
        block = place_ref[1] ^ step
        total[...] = jnp.zeros_like(total)
        for slot in range(SLOTS):
            row = index_ref[step, slot]
            col = index_ref[step, SLOTS + slot]
            valid = index_ref[step, 2 * SLOTS + slot]
            tile = tiles_refs[step][slot * TILE : (slot + 1) * TILE, :]
            product = jnp.dot(tile, panel_ref[col], preferred_element_type=F32)
            total[row] += jnp.where(valid > 0, product, 0.0)
        for pair in range(Z):
            mine_ref[block * Z + pair] = total[2 * pair + core].astype(BF16)
            other_ref[block * Z + pair] = total[2 * pair + 1 - core].astype(BF16)


def middle(core_ref, parts_ref, weight_ref, cotangent_ref, act_ref, grad_ref, keep_ref, send_ref):
    chunks = []
    for chunk in range(X):
        total = parts_ref[chunk * Z].astype(F32)
        for z in range(1, Z):
            total += parts_ref[chunk * Z + z].astype(F32)
        chunks.append(total)
    summed = jnp.concatenate(chunks, axis=1)
    high = summed.astype(BF16)
    low = (summed - high.astype(F32)).astype(BF16)
    weight = weight_ref[...]
    aggregated = jnp.dot(high, weight, preferred_element_type=F32) + jnp.dot(
        low, weight, preferred_element_type=F32
    )
    sig = jax.nn.sigmoid(aggregated)
    act_ref[...] = (aggregated * sig).astype(BF16)
    grad = (cotangent_ref[...].astype(F32) * sig * (1.0 + aggregated * (1.0 - sig))).astype(BF16)
    for chunk in range(X):
        piece = grad[:, chunk * CHUNK : (chunk + 1) * CHUNK]
        for z in range(Z):
            grad_ref[chunk * Z + z] = piece
    weight_part = lax.dot_general(
        high, grad, (((0,), (0,)), ((), ())), preferred_element_type=F32
    ).astype(BF16)
    low_half, high_half = weight_part[: WIDTH // 2], weight_part[WIDTH // 2 :]
    upper = core_ref[0] == 1
    keep_ref[...] = jnp.where(upper, high_half, low_half)
    send_ref[...] = jnp.where(upper, low_half, high_half)


def backward_tiles(place_ref, index_ref, mine_ref, other_ref, *refs):
    tiles_refs, (out_ref, total) = refs[:X], refs[X:]
    core = place_ref[0]
    total[...] = jnp.zeros_like(total)
    for step in range(X):
        block = place_ref[1] ^ step
        for slot in range(SLOTS):
            row = index_ref[step, slot]
            col = index_ref[step, SLOTS + slot]
            valid = index_ref[step, 2 * SLOTS + slot]
            at = block * Z + row // 2
            panel = jnp.where(row % 2 == core, mine_ref[at], other_ref[at])
            tile = tiles_refs[step][slot * TILE : (slot + 1) * TILE, :]
            product = lax.dot_general(
                tile, panel, (((0,), (0,)), ((), ())), preferred_element_type=F32
            )
            total[col] += jnp.where(valid > 0, product, 0.0)
    for tile in range(COL_TILES):
        out_ref[tile] = total[tile].astype(BF16)


def last(parts_ref, weight_ref, out_ref):
    chunks = []
    for chunk in range(X):
        total = parts_ref[chunk].astype(F32)
        for y in range(1, Y):
            total += parts_ref[y * X + chunk].astype(F32)
        chunks.append(total)
    summed = jnp.concatenate(chunks, axis=1).astype(BF16)
    out_ref[...] = lax.dot_general(
        summed, weight_ref[...], (((1,), (1,)), ((), ())), preferred_element_type=F32
    ).astype(BF16)


def place_rows(place_ref, mine_ref, other_ref, out_ref):
    core = place_ref[0]
    half, share = WIDTH // CORES, WIDTH // (Y * CORES)
    scale = 1.0 / math.sqrt(TILE * Y * X * Z * CORES)
    for y in range(Y):
        at = (y & 1) * 4 * share + (y >> 1 & 1) * 2 * share + (y >> 2) * share
        for side, ref in ((core, mine_ref), (1 - core, other_ref)):
            start = pl.multiple_of(side * half + at, share)
            out_ref[pl.ds(start, share), :] = ref[y].astype(F32) * scale


def exchange(array, axis, distance):
    size = lax.axis_size(axis)
    return lax.ppermute(array, axis, [(i, i ^ distance) for i in range(size)])


def halve(array, axis, distance):
    upper = jnp.minimum(lax.axis_index(axis) & distance, 1)
    halves = array.reshape(2, array.shape[0] // 2, array.shape[1])
    send = lax.dynamic_index_in_dim(halves, 1 - upper, 0, keepdims=False)
    keep = lax.dynamic_index_in_dim(halves, upper, 0, keepdims=False)
    return (keep.astype(F32) + exchange(send, axis, distance).astype(F32)).astype(BF16)


def double(array, axis, distance):
    return (array.astype(F32) + exchange(array, axis, distance).astype(F32)).astype(BF16)


def body(features, weight, cotangent, tile_values, tile_rows, tile_cols, tile_valid):
    place = jnp.stack([lax.axis_index("core"), lax.axis_index("x")]).astype(jnp.int32)

    chunks = pl.pallas_call(
        spread,
        in_specs=[vmem()],
        out_specs=vmem(),
        out_shape=jax.ShapeDtypeStruct((COL_TILES, TILE, CHUNK), BF16),
        compiler_params=params(),
        name="spread",
    )(features)
    panel = lax.all_to_all(chunks, ("y", "x"), 0, 0, tiled=True)

    tiles = tile_values.reshape(SLOTS * TILE, TILE)
    tiles = [tiles] + [exchange(tiles, "x", distance) for distance in range(1, X)]
    index = jnp.concatenate([tile_rows, tile_cols, tile_valid], axis=2).reshape(1, 3 * SLOTS)
    for distance in (1, 2):
        index = jnp.concatenate([index, exchange(index, "x", distance)])

    mine, other = pl.pallas_call(
        forward_tiles,
        in_specs=[smem(), smem()] + [vmem()] * (1 + X),
        out_specs=[vmem()] * 2,
        out_shape=[jax.ShapeDtypeStruct((X * Z, TILE, CHUNK), BF16)] * 2,
        scratch_shapes=[pltpu.VMEM((ROW_TILES, TILE, CHUNK), F32)],
        compiler_params=params(),
        name="forward_tiles",
    )(place, index, panel, *tiles)
    term = (mine.astype(F32) + exchange(other, "core", 1).astype(F32)).astype(BF16)
    parts = lax.all_to_all(term, ("x", "z"), 0, 0, tiled=True)

    half = WIDTH // CORES
    activations, grad, weight_keep, weight_send = pl.pallas_call(
        middle,
        in_specs=[smem()] + [vmem()] * 3,
        out_specs=[vmem()] * 4,
        out_shape=[
            jax.ShapeDtypeStruct((TILE, WIDTH), BF16),
            jax.ShapeDtypeStruct((X * Z, TILE, CHUNK), BF16),
            jax.ShapeDtypeStruct((half, WIDTH), BF16),
            jax.ShapeDtypeStruct((half, WIDTH), BF16),
        ],
        compiler_params=params(),
        name="middle",
    )(place, parts, weight, cotangent)

    grad_mine = lax.all_to_all(grad, ("x", "z"), 0, 0, tiled=True)
    piece = weight_keep.astype(F32) + exchange(weight_send, "core", 1).astype(F32)
    piece = piece.astype(BF16)
    for distance in (1, 2, 4):
        piece = halve(piece, "y", distance)
    grad_mine, piece = lax.optimization_barrier((grad_mine, piece))

    grad_other = exchange(grad_mine, "core", 1)
    piece = double(piece, "z", 1)
    grad_mine, grad_other, piece = lax.optimization_barrier((grad_mine, grad_other, piece))
    piece = double(piece, "z", 2)
    back = pl.pallas_call(
        backward_tiles,
        in_specs=[smem(), smem()] + [vmem()] * (2 + X),
        out_specs=vmem(),
        out_shape=jax.ShapeDtypeStruct((COL_TILES, TILE, CHUNK), BF16),
        scratch_shapes=[pltpu.VMEM((COL_TILES, TILE, CHUNK), F32)],
        compiler_params=params(),
        name="backward_tiles",
    )(place, index, grad_mine, grad_other, *tiles)
    back, piece = lax.optimization_barrier((back, piece))
    back = lax.all_to_all(back, ("y", "x"), 0, 0, tiled=True)
    for axis, distance in (("z", 4), ("x", 1), ("x", 2)):
        piece = double(piece, axis, distance)
    back, piece = lax.optimization_barrier((back, piece))

    input_grad = pl.pallas_call(
        last,
        in_specs=[vmem()] * 2,
        out_specs=vmem(),
        out_shape=jax.ShapeDtypeStruct((TILE, WIDTH), BF16),
        compiler_params=params(),
        name="last",
    )(back, weight)

    share = WIDTH // (Y * CORES)
    piece = jnp.broadcast_to(piece[None], (Y, share, WIDTH))
    whole = lax.all_to_all(piece, "y", 0, 0, tiled=True)
    weight_grad = pl.pallas_call(
        place_rows,
        in_specs=[smem()] + [vmem()] * 2,
        out_specs=vmem(),
        out_shape=jax.ShapeDtypeStruct((WIDTH, WIDTH), F32),
        compiler_params=params(),
        name="place_rows",
    )(place, whole, exchange(whole, "core", 1))
    return (activations, input_grad, weight_grad)


def solution(mesh):
    axes = Mesh(mesh.devices.reshape(Y, X, Z, CORES), ("y", "x", "z", "core"))
    row, col = ("y", "x"), ("z", "core")
    placed = (
        P(col + row, None),
        P(),
        P(row + col, None),
        P(row, col, None, None, None),
        P(row, col, None),
        P(row, col, None),
        P(row, col, None),
    )
    return jax.shard_map(
        body,
        mesh=axes,
        in_specs=placed,
        out_specs=(P(row + col, None), P(col + row, None), P()),
        check_vma=False,
    )
```

```python
import math

import jax
import jax.numpy as jnp
from jax import lax
from jax.experimental import pallas as pl
from jax.experimental.pallas import tpu as pltpu
from jax.sharding import Mesh, PartitionSpec as P

Y, X, Z, CORES = 8, 4, 8, 2
TILE = 128
SLOTS = 8
WIDTH = 512
CHUNK = WIDTH // X
ROW_TILES = Z * CORES
COL_TILES = Y * X
INDEX_ROWS = 16
BF16 = jnp.bfloat16
F32 = jnp.float32


def params():
    return pltpu.CompilerParams(vmem_limit_bytes=24 * 1024 * 1024)


def vmem():
    return pl.BlockSpec(memory_space=pltpu.VMEM)


def smem():
    return pl.BlockSpec(memory_space=pltpu.SMEM)


def spread(features_ref, out_ref):
    for chunk in range(X):
        piece = features_ref[:, chunk * CHUNK : (chunk + 1) * CHUNK]
        for y in range(Y):
            out_ref[y * X + chunk] = piece


def forward_tiles(place_ref, index_ref, panel_ref, *refs):
    tiles_refs, (mine_ref, other_ref, total) = refs[:X], refs[X:]
    core = place_ref[0]
    for step in range(X):
        block = place_ref[1] ^ step
        total[...] = jnp.zeros_like(total)
        for slot in range(SLOTS):
            row = index_ref[step, slot]
            col = index_ref[step, SLOTS + slot]
            valid = index_ref[step, 2 * SLOTS + slot]
            tile = tiles_refs[step][slot * TILE : (slot + 1) * TILE, :]
            product = jnp.dot(tile, panel_ref[col], preferred_element_type=F32)
            total[row] += jnp.where(valid > 0, product, 0.0)
        for pair in range(Z):
            mine_ref[block * Z + pair] = total[2 * pair + core].astype(BF16)
            other_ref[block * Z + pair] = total[2 * pair + 1 - core].astype(BF16)


def middle(parts_ref, weight_ref, cotangent_ref, act_ref, grad_ref, weight_part_ref):
    chunks = []
    for chunk in range(X):
        total = parts_ref[chunk * Z].astype(F32)
        for z in range(1, Z):
            total += parts_ref[chunk * Z + z].astype(F32)
        chunks.append(total)
    summed = jnp.concatenate(chunks, axis=1)
    high = summed.astype(BF16)
    low = (summed - high.astype(F32)).astype(BF16)
    weight = weight_ref[...]
    aggregated = jnp.dot(high, weight, preferred_element_type=F32) + jnp.dot(
        low, weight, preferred_element_type=F32
    )
    sig = jax.nn.sigmoid(aggregated)
    act_ref[...] = (aggregated * sig).astype(BF16)
    grad = (cotangent_ref[...].astype(F32) * sig * (1.0 + aggregated * (1.0 - sig))).astype(BF16)
    for chunk in range(X):
        piece = grad[:, chunk * CHUNK : (chunk + 1) * CHUNK]
        for z in range(Z):
            grad_ref[chunk * Z + z] = piece
    weight_part_ref[...] = lax.dot_general(
        high, grad, (((0,), (0,)), ((), ())), preferred_element_type=F32
    ).astype(BF16)


def backward_tiles(place_ref, index_ref, mine_ref, other_ref, *refs):
    tiles_refs, (out_ref, total) = refs[:X], refs[X:]
    core = place_ref[0]
    total[...] = jnp.zeros_like(total)
    for step in range(X):
        block = place_ref[1] ^ step
        for slot in range(SLOTS):
            row = index_ref[step, slot]
            col = index_ref[step, SLOTS + slot]
            valid = index_ref[step, 2 * SLOTS + slot]
            at = block * Z + row // 2
            panel = jnp.where(row % 2 == core, mine_ref[at], other_ref[at])
            tile = tiles_refs[step][slot * TILE : (slot + 1) * TILE, :]
            product = lax.dot_general(
                tile, panel, (((0,), (0,)), ((), ())), preferred_element_type=F32
            )
            total[col] += jnp.where(valid > 0, product, 0.0)
    for tile in range(COL_TILES):
        out_ref[tile] = total[tile].astype(BF16)


def last(parts_ref, weight_ref, out_ref):
    chunks = []
    for chunk in range(X):
        total = parts_ref[chunk].astype(F32)
        for y in range(1, Y):
            total += parts_ref[y * X + chunk].astype(F32)
        chunks.append(total)
    summed = jnp.concatenate(chunks, axis=1).astype(BF16)
    out_ref[...] = lax.dot_general(
        summed, weight_ref[...], (((1,), (1,)), ((), ())), preferred_element_type=F32
    ).astype(BF16)


def place_rows(pieces_ref, out_ref):
    share = WIDTH // Y
    scale = 1.0 / math.sqrt(TILE * Y * X * Z * CORES)
    for y in range(Y):
        at = ((y & 1) * 4 + (y >> 1 & 1) * 2 + (y >> 2)) * share
        out_ref[at : at + share, :] = pieces_ref[y].astype(F32) * scale


def exchange(array, axis, distance):
    size = lax.axis_size(axis)
    return lax.ppermute(array, axis, [(i, i ^ distance) for i in range(size)])


def halve(array, axis, distance):
    upper = jnp.minimum(lax.axis_index(axis) & distance, 1)
    halves = array.reshape(2, array.shape[0] // 2, array.shape[1])
    send = lax.dynamic_index_in_dim(halves, 1 - upper, 0, keepdims=False)
    keep = lax.dynamic_index_in_dim(halves, upper, 0, keepdims=False)
    return (keep.astype(F32) + exchange(send, axis, distance).astype(F32)).astype(BF16)


def double(array, axis, distance):
    return (array.astype(F32) + exchange(array, axis, distance).astype(F32)).astype(BF16)


def body(features, weight, cotangent, tile_values, tile_rows, tile_cols, tile_valid):
    place = jnp.stack([lax.axis_index("core"), lax.axis_index("x")]).astype(jnp.int32)

    chunks = pl.pallas_call(
        spread,
        in_specs=[vmem()],
        out_specs=vmem(),
        out_shape=jax.ShapeDtypeStruct((COL_TILES, TILE, CHUNK), BF16),
        compiler_params=params(),
        name="spread",
    )(features)
    panel = lax.all_to_all(chunks, ("y", "x"), 0, 0, tiled=True)

    index = jnp.concatenate(
        [tile_rows.reshape(-1), tile_cols.reshape(-1), tile_valid.reshape(-1)]
    ).astype(BF16)
    index = jnp.pad(index[None, :], ((0, INDEX_ROWS - 1), (0, TILE - 3 * SLOTS)))
    tiles = jnp.concatenate([tile_values.reshape(SLOTS * TILE, TILE), index], axis=0)
    tiles = [tiles] + [exchange(tiles, "x", distance) for distance in range(1, X)]
    index = jnp.stack([t[SLOTS * TILE, : 3 * SLOTS] for t in tiles]).astype(jnp.int32)
    limit = jnp.repeat(jnp.array([ROW_TILES - 1, COL_TILES - 1, 1], jnp.int32), SLOTS)
    index = jnp.clip(index, 0, limit[None, :])

    mine, other = pl.pallas_call(
        forward_tiles,
        in_specs=[smem(), smem()] + [vmem()] * (1 + X),
        out_specs=[vmem()] * 2,
        out_shape=[jax.ShapeDtypeStruct((X * Z, TILE, CHUNK), BF16)] * 2,
        scratch_shapes=[pltpu.VMEM((ROW_TILES, TILE, CHUNK), F32)],
        compiler_params=params(),
        name="forward_tiles",
    )(place, index, panel, *tiles)
    term = (mine.astype(F32) + exchange(other, "core", 1).astype(F32)).astype(BF16)
    parts = lax.all_to_all(term, ("x", "z"), 0, 0, tiled=True)

    activations, grad, piece = pl.pallas_call(
        middle,
        in_specs=[vmem()] * 3,
        out_specs=[vmem()] * 3,
        out_shape=[
            jax.ShapeDtypeStruct((TILE, WIDTH), BF16),
            jax.ShapeDtypeStruct((X * Z, TILE, CHUNK), BF16),
            jax.ShapeDtypeStruct((WIDTH, WIDTH), BF16),
        ],
        compiler_params=params(),
        name="middle",
    )(parts, weight, cotangent)

    grad_mine = lax.all_to_all(grad, ("x", "z"), 0, 0, tiled=True)
    for distance in (1, 2, 4):
        piece = halve(piece, "y", distance)
    piece = double(piece, "z", 1)
    grad_mine, piece = lax.optimization_barrier((grad_mine, piece))

    grad_other = exchange(grad_mine, "core", 1)
    piece = double(piece, "z", 2)
    back = pl.pallas_call(
        backward_tiles,
        in_specs=[smem(), smem()] + [vmem()] * (2 + X),
        out_specs=vmem(),
        out_shape=jax.ShapeDtypeStruct((COL_TILES, TILE, CHUNK), BF16),
        scratch_shapes=[pltpu.VMEM((COL_TILES, TILE, CHUNK), F32)],
        compiler_params=params(),
        name="backward_tiles",
    )(place, index, grad_mine, grad_other, *tiles)
    back, piece = lax.optimization_barrier((back, piece))
    back = lax.all_to_all(back, ("y", "x"), 0, 0, tiled=True)
    piece = double(piece, "z", 4)
    piece = lax.all_gather(piece, ("x", "core"), axis=0).astype(F32).sum(0).astype(BF16)
    back, piece = lax.optimization_barrier((back, piece))

    input_grad = pl.pallas_call(
        last,
        in_specs=[vmem()] * 2,
        out_specs=vmem(),
        out_shape=jax.ShapeDtypeStruct((TILE, WIDTH), BF16),
        compiler_params=params(),
        name="last",
    )(back, weight)

    piece = jnp.broadcast_to(piece[None], (Y, WIDTH // Y, WIDTH))
    whole = lax.all_to_all(piece, "y", 0, 0, tiled=True)
    weight_grad = pl.pallas_call(
        place_rows,
        in_specs=[vmem()],
        out_specs=vmem(),
        out_shape=jax.ShapeDtypeStruct((WIDTH, WIDTH), F32),
        compiler_params=params(),
        name="place_rows",
    )(whole)
    return (activations, input_grad, weight_grad)


def solution(mesh):
    axes = Mesh(mesh.devices.reshape(Y, X, Z, CORES), ("y", "x", "z", "core"))
    row, col = ("y", "x"), ("z", "core")
    placed = (
        P(col + row, None),
        P(),
        P(row + col, None),
        P(row, col, None, None, None),
        P(row, col, None),
        P(row, col, None),
        P(row, col, None),
    )
    return jax.shard_map(
        body,
        mesh=axes,
        in_specs=placed,
        out_specs=(P(row + col, None), P(col + row, None), P()),
        check_vma=False,
    )
```

```python
import math

import jax
import jax.numpy as jnp
from jax import lax
from jax.experimental import pallas as pl
from jax.experimental.pallas import tpu as pltpu
from jax.sharding import Mesh, PartitionSpec as P

Y, X, Z, CORES = 8, 4, 8, 2
TILE = 128
SLOTS = 8
WIDTH = 512
CHUNK = WIDTH // X
ROW_TILES = Z * CORES
COL_TILES = Y * X
INDEX_ROWS = 16
BF16 = jnp.bfloat16
F32 = jnp.float32


def params():
    return pltpu.CompilerParams(vmem_limit_bytes=24 * 1024 * 1024)


def vmem():
    return pl.BlockSpec(memory_space=pltpu.VMEM)


def smem():
    return pl.BlockSpec(memory_space=pltpu.SMEM)


def spread(features_ref, out_ref):
    for chunk in range(X):
        piece = features_ref[:, chunk * CHUNK : (chunk + 1) * CHUNK]
        for y in range(Y):
            out_ref[y * X + chunk] = piece


def forward_tiles(place_ref, index_ref, panel_ref, *refs):
    tiles_refs, (mine_ref, other_ref, total) = refs[:X], refs[X:]
    core = place_ref[0]
    for step in range(X):
        block = place_ref[1] ^ step
        total[...] = jnp.zeros_like(total)
        for slot in range(SLOTS):
            row = index_ref[step, slot]
            col = index_ref[step, SLOTS + slot]
            valid = index_ref[step, 2 * SLOTS + slot]
            tile = tiles_refs[step][slot * TILE : (slot + 1) * TILE, :]
            product = jnp.dot(tile, panel_ref[col], preferred_element_type=F32)
            total[row] += jnp.where(valid > 0, product, 0.0)
        for pair in range(Z):
            mine_ref[block * Z + pair] = total[2 * pair + core].astype(BF16)
            other_ref[block * Z + pair] = total[2 * pair + 1 - core].astype(BF16)


def middle(core_ref, parts_ref, weight_ref, cotangent_ref, act_ref, grad_ref, keep_ref, send_ref):
    chunks = []
    for chunk in range(X):
        total = parts_ref[chunk * Z].astype(F32)
        for z in range(1, Z):
            total += parts_ref[chunk * Z + z].astype(F32)
        chunks.append(total)
    summed = jnp.concatenate(chunks, axis=1)
    high = summed.astype(BF16)
    low = (summed - high.astype(F32)).astype(BF16)
    weight = weight_ref[...]
    aggregated = jnp.dot(high, weight, preferred_element_type=F32) + jnp.dot(
        low, weight, preferred_element_type=F32
    )
    sig = jax.nn.sigmoid(aggregated)
    act_ref[...] = (aggregated * sig).astype(BF16)
    grad = (cotangent_ref[...].astype(F32) * sig * (1.0 + aggregated * (1.0 - sig))).astype(BF16)
    for chunk in range(X):
        piece = grad[:, chunk * CHUNK : (chunk + 1) * CHUNK]
        for z in range(Z):
            grad_ref[chunk * Z + z] = piece
    weight_part = lax.dot_general(
        high, grad, (((0,), (0,)), ((), ())), preferred_element_type=F32
    ).astype(BF16)
    low_half, high_half = weight_part[: WIDTH // 2], weight_part[WIDTH // 2 :]
    upper = core_ref[0] == 1
    keep_ref[...] = jnp.where(upper, high_half, low_half)
    send_ref[...] = jnp.where(upper, low_half, high_half)


def backward_tiles(place_ref, index_ref, mine_ref, other_ref, *refs):
    tiles_refs, (out_ref, total) = refs[:X], refs[X:]
    core = place_ref[0]
    total[...] = jnp.zeros_like(total)
    for step in range(X):
        block = place_ref[1] ^ step
        for slot in range(SLOTS):
            row = index_ref[step, slot]
            col = index_ref[step, SLOTS + slot]
            valid = index_ref[step, 2 * SLOTS + slot]
            at = block * Z + row // 2
            panel = jnp.where(row % 2 == core, mine_ref[at], other_ref[at])
            tile = tiles_refs[step][slot * TILE : (slot + 1) * TILE, :]
            product = lax.dot_general(
                tile, panel, (((0,), (0,)), ((), ())), preferred_element_type=F32
            )
            total[col] += jnp.where(valid > 0, product, 0.0)
    for tile in range(COL_TILES):
        out_ref[tile] = total[tile].astype(BF16)


def last(parts_ref, weight_ref, out_ref):
    chunks = []
    for chunk in range(X):
        total = parts_ref[chunk].astype(F32)
        for y in range(1, Y):
            total += parts_ref[y * X + chunk].astype(F32)
        chunks.append(total)
    summed = jnp.concatenate(chunks, axis=1).astype(BF16)
    out_ref[...] = lax.dot_general(
        summed, weight_ref[...], (((1,), (1,)), ((), ())), preferred_element_type=F32
    ).astype(BF16)


def place_rows(place_ref, mine_ref, other_ref, out_ref):
    core = place_ref[0]
    half, share = WIDTH // CORES, WIDTH // (Y * CORES)
    scale = 1.0 / math.sqrt(TILE * Y * X * Z * CORES)
    for y in range(Y):
        at = (y & 1) * 4 * share + (y >> 1 & 1) * 2 * share + (y >> 2) * share
        for side, ref in ((core, mine_ref), (1 - core, other_ref)):
            start = pl.multiple_of(side * half + at, share)
            out_ref[pl.ds(start, share), :] = ref[y].astype(F32) * scale


def exchange(array, axis, distance):
    size = lax.axis_size(axis)
    return lax.ppermute(array, axis, [(i, i ^ distance) for i in range(size)])


def halve(array, axis, distance):
    upper = jnp.minimum(lax.axis_index(axis) & distance, 1)
    halves = array.reshape(2, array.shape[0] // 2, array.shape[1])
    send = lax.dynamic_index_in_dim(halves, 1 - upper, 0, keepdims=False)
    keep = lax.dynamic_index_in_dim(halves, upper, 0, keepdims=False)
    return (keep.astype(F32) + exchange(send, axis, distance).astype(F32)).astype(BF16)


def double(array, axis, distance):
    return (array.astype(F32) + exchange(array, axis, distance).astype(F32)).astype(BF16)


def body(features, weight, cotangent, tile_values, tile_rows, tile_cols, tile_valid):
    place = jnp.stack([lax.axis_index("core"), lax.axis_index("x")]).astype(jnp.int32)

    chunks = pl.pallas_call(
        spread,
        in_specs=[vmem()],
        out_specs=vmem(),
        out_shape=jax.ShapeDtypeStruct((COL_TILES, TILE, CHUNK), BF16),
        compiler_params=params(),
        name="spread",
    )(features)
    panel = lax.all_to_all(chunks, ("y", "x"), 0, 0, tiled=True)

    index = jnp.concatenate(
        [tile_rows.reshape(-1), tile_cols.reshape(-1), tile_valid.reshape(-1)]
    ).astype(BF16)
    index = jnp.pad(index[None, :], ((0, INDEX_ROWS - 1), (0, TILE - 3 * SLOTS)))
    tiles = jnp.concatenate([tile_values.reshape(SLOTS * TILE, TILE), index], axis=0)
    tiles = [tiles] + [exchange(tiles, "x", distance) for distance in range(1, X)]
    index = jnp.stack([t[SLOTS * TILE, : 3 * SLOTS] for t in tiles]).astype(jnp.int32)
    limit = jnp.repeat(jnp.array([ROW_TILES - 1, COL_TILES - 1, 1], jnp.int32), SLOTS)
    index = jnp.clip(index, 0, limit[None, :])

    mine, other = pl.pallas_call(
        forward_tiles,
        in_specs=[smem(), smem()] + [vmem()] * (1 + X),
        out_specs=[vmem()] * 2,
        out_shape=[jax.ShapeDtypeStruct((X * Z, TILE, CHUNK), BF16)] * 2,
        scratch_shapes=[pltpu.VMEM((ROW_TILES, TILE, CHUNK), F32)],
        compiler_params=params(),
        name="forward_tiles",
    )(place, index, panel, *tiles)
    term = (mine.astype(F32) + exchange(other, "core", 1).astype(F32)).astype(BF16)
    parts = lax.all_to_all(term, ("x", "z"), 0, 0, tiled=True)

    half = WIDTH // CORES
    activations, grad, weight_keep, weight_send = pl.pallas_call(
        middle,
        in_specs=[smem()] + [vmem()] * 3,
        out_specs=[vmem()] * 4,
        out_shape=[
            jax.ShapeDtypeStruct((TILE, WIDTH), BF16),
            jax.ShapeDtypeStruct((X * Z, TILE, CHUNK), BF16),
            jax.ShapeDtypeStruct((half, WIDTH), BF16),
            jax.ShapeDtypeStruct((half, WIDTH), BF16),
        ],
        compiler_params=params(),
        name="middle",
    )(place, parts, weight, cotangent)

    grad_mine = lax.all_to_all(grad, ("x", "z"), 0, 0, tiled=True)
    piece = weight_keep.astype(F32) + exchange(weight_send, "core", 1).astype(F32)
    piece = piece.astype(BF16)
    for distance in (1, 2, 4):
        piece = halve(piece, "y", distance)
    grad_mine, piece = lax.optimization_barrier((grad_mine, piece))

    grad_other = exchange(grad_mine, "core", 1)
    piece = double(piece, "z", 1)
    back = pl.pallas_call(
        backward_tiles,
        in_specs=[smem(), smem()] + [vmem()] * (2 + X),
        out_specs=vmem(),
        out_shape=jax.ShapeDtypeStruct((COL_TILES, TILE, CHUNK), BF16),
        scratch_shapes=[pltpu.VMEM((COL_TILES, TILE, CHUNK), F32)],
        compiler_params=params(),
        name="backward_tiles",
    )(place, index, grad_mine, grad_other, *tiles)
    back, piece = lax.optimization_barrier((back, piece))
    back = lax.all_to_all(back, ("y", "x"), 0, 0, tiled=True)
    for distance in (2, 4):
        piece = double(piece, "z", distance)
    piece = lax.all_gather(piece, "x", axis=0).astype(F32).sum(0).astype(BF16)
    back, piece = lax.optimization_barrier((back, piece))

    input_grad = pl.pallas_call(
        last,
        in_specs=[vmem()] * 2,
        out_specs=vmem(),
        out_shape=jax.ShapeDtypeStruct((TILE, WIDTH), BF16),
        compiler_params=params(),
        name="last",
    )(back, weight)

    share = WIDTH // (Y * CORES)
    piece = jnp.broadcast_to(piece[None], (Y, share, WIDTH))
    whole = lax.all_to_all(piece, "y", 0, 0, tiled=True)
    weight_grad = pl.pallas_call(
        place_rows,
        in_specs=[smem()] + [vmem()] * 2,
        out_specs=vmem(),
        out_shape=jax.ShapeDtypeStruct((WIDTH, WIDTH), F32),
        compiler_params=params(),
        name="place_rows",
    )(place, whole, exchange(whole, "core", 1))
    return (activations, input_grad, weight_grad)


def solution(mesh):
    axes = Mesh(mesh.devices.reshape(Y, X, Z, CORES), ("y", "x", "z", "core"))
    row, col = ("y", "x"), ("z", "core")
    placed = (
        P(col + row, None),
        P(),
        P(row + col, None),
        P(row, col, None, None, None),
        P(row, col, None),
        P(row, col, None),
        P(row, col, None),
    )
    return jax.shard_map(
        body,
        mesh=axes,
        in_specs=placed,
        out_specs=(P(row + col, None), P(col + row, None), P()),
        check_vma=False,
    )
```

```python
import math

import jax
import jax.numpy as jnp
from jax import lax
from jax.experimental import pallas as pl
from jax.experimental.pallas import tpu as pltpu
from jax.sharding import Mesh, PartitionSpec as P

Y, X, Z, CORES = 8, 4, 8, 2
TILE = 128
SLOTS = 8
WIDTH = 512
CHUNK = WIDTH // X
HALF = CHUNK // CORES
ROW_TILES = Z * CORES
COL_TILES = Y * X
INDEX_ROWS = 16
BF16 = jnp.bfloat16
F32 = jnp.float32


def params():
    return pltpu.CompilerParams(vmem_limit_bytes=24 * 1024 * 1024)


def vmem():
    return pl.BlockSpec(memory_space=pltpu.VMEM)


def smem():
    return pl.BlockSpec(memory_space=pltpu.SMEM)


def spread(features_ref, out_ref):
    for chunk in range(X):
        piece = features_ref[:, chunk * CHUNK : (chunk + 1) * CHUNK]
        for y in range(Y):
            out_ref[y * X + chunk] = piece


def forward_tiles(place_ref, index_ref, panel_ref, *refs):
    tiles_refs, (mine_ref, other_ref, total) = refs[:X], refs[X:]
    core = place_ref[0]
    for step in range(X):
        block = place_ref[1] ^ step
        total[...] = jnp.zeros_like(total)
        for slot in range(SLOTS):
            row = index_ref[step, slot]
            col = index_ref[step, SLOTS + slot]
            valid = index_ref[step, 2 * SLOTS + slot]
            tile = tiles_refs[step][slot * TILE : (slot + 1) * TILE, :]
            product = jnp.dot(tile, panel_ref[col], preferred_element_type=F32)
            total[row] += jnp.where(valid > 0, product, 0.0)
        for pair in range(Z):
            mine_ref[block * Z + pair] = total[2 * pair + core].astype(BF16)
            other_ref[block * Z + pair] = total[2 * pair + 1 - core].astype(BF16)


def split_lanes(tile):
    rows = TILE // 2
    top, bottom = tile[:rows], tile[rows:]
    left = jnp.concatenate([top[:, :HALF], bottom[:, :HALF]], axis=1)
    right = jnp.concatenate([top[:, HALF:], bottom[:, HALF:]], axis=1)
    return left, right


def join_lanes(left, right):
    top = jnp.concatenate([left[:, :HALF], right[:, :HALF]], axis=1)
    bottom = jnp.concatenate([left[:, HALF:], right[:, HALF:]], axis=1)
    return jnp.concatenate([top, bottom], axis=0)


def middle(core_ref, parts_ref, weight_ref, cotangent_ref, act_ref, grad_ref, keep_ref, send_ref):
    chunks = []
    for chunk in range(X):
        total = parts_ref[chunk * Z].astype(F32)
        for z in range(1, Z):
            total += parts_ref[chunk * Z + z].astype(F32)
        chunks.append(total)
    summed = jnp.concatenate(chunks, axis=1)
    high = summed.astype(BF16)
    low = (summed - high.astype(F32)).astype(BF16)
    weight = weight_ref[...]
    aggregated = jnp.dot(high, weight, preferred_element_type=F32) + jnp.dot(
        low, weight, preferred_element_type=F32
    )
    sig = jax.nn.sigmoid(aggregated)
    act_ref[...] = (aggregated * sig).astype(BF16)
    grad = (cotangent_ref[...].astype(F32) * sig * (1.0 + aggregated * (1.0 - sig))).astype(BF16)
    for chunk in range(X):
        both = grad[:, chunk * CHUNK : (chunk + 1) * CHUNK]
        for core, piece in enumerate(split_lanes(both)):
            for z in range(Z):
                grad_ref[(chunk * Z + z) * CORES + core] = piece
    weight_part = lax.dot_general(
        high, grad, (((0,), (0,)), ((), ())), preferred_element_type=F32
    ).astype(BF16)
    low_half, high_half = weight_part[: WIDTH // 2], weight_part[WIDTH // 2 :]
    upper = core_ref[0] == 1
    keep_ref[...] = jnp.where(upper, high_half, low_half)
    send_ref[...] = jnp.where(upper, low_half, high_half)


def backward_tiles(place_ref, index_ref, grad_ref, *refs):
    tiles_refs, (out_ref, panel, total) = refs[: CORES * X], refs[CORES * X :]
    for tile in range(X * ROW_TILES):
        piece = grad_ref[tile]
        panel[tile] = join_lanes(piece, piece)
    total[...] = jnp.zeros_like(total)
    right = lax.broadcasted_iota(jnp.int32, (TILE, CHUNK), 1) // HALF
    for step in range(CORES * X):
        core = place_ref[0] ^ (step // X)
        block = place_ref[1] ^ (step % X)
        mine = right == core
        for slot in range(SLOTS):
            row = index_ref[step, slot]
            col = index_ref[step, SLOTS + slot]
            valid = index_ref[step, 2 * SLOTS + slot]
            tile = tiles_refs[step][slot * TILE : (slot + 1) * TILE, :]
            product = lax.dot_general(
                tile, panel[block * ROW_TILES + row], (((0,), (0,)), ((), ())), preferred_element_type=F32
            )
            total[col] += jnp.where(mine & (valid > 0), product, 0.0)
    for tile in range(COL_TILES):
        for core, piece in enumerate(split_lanes(total[tile].astype(BF16))):
            out_ref[tile * CORES + core] = piece


def last(parts_ref, weight_ref, out_ref):
    chunks = []
    for chunk in range(X):
        halves = []
        for core in range(CORES):
            total = parts_ref[chunk * CORES + core].astype(F32)
            for y in range(1, Y):
                total += parts_ref[(y * X + chunk) * CORES + core].astype(F32)
            halves.append(total)
        chunks.append(join_lanes(*halves))
    summed = jnp.concatenate(chunks, axis=1).astype(BF16)
    out_ref[...] = lax.dot_general(
        summed, weight_ref[...], (((1,), (1,)), ((), ())), preferred_element_type=F32
    ).astype(BF16)


def place_rows(place_ref, mine_ref, other_ref, out_ref):
    core = place_ref[0]
    half, share = WIDTH // CORES, WIDTH // (Y * CORES)
    scale = 1.0 / math.sqrt(TILE * Y * X * Z * CORES)
    for y in range(Y):
        at = (y & 1) * 4 * share + (y >> 1 & 1) * 2 * share + (y >> 2) * share
        for side, ref in ((core, mine_ref), (1 - core, other_ref)):
            start = pl.multiple_of(side * half + at, share)
            out_ref[pl.ds(start, share), :] = ref[y].astype(F32) * scale


def exchange(array, axis, distance):
    size = lax.axis_size(axis)
    return lax.ppermute(array, axis, [(i, i ^ distance) for i in range(size)])


def halve(array, axis, distance):
    upper = jnp.minimum(lax.axis_index(axis) & distance, 1)
    halves = array.reshape(2, array.shape[0] // 2, array.shape[1])
    send = lax.dynamic_index_in_dim(halves, 1 - upper, 0, keepdims=False)
    keep = lax.dynamic_index_in_dim(halves, upper, 0, keepdims=False)
    return (keep.astype(F32) + exchange(send, axis, distance).astype(F32)).astype(BF16)


def double(array, axis, distance):
    return (array.astype(F32) + exchange(array, axis, distance).astype(F32)).astype(BF16)


def slots_of(tiles):
    index = jnp.stack([t[SLOTS * TILE, : 3 * SLOTS] for t in tiles]).astype(jnp.int32)
    limit = jnp.repeat(jnp.array([ROW_TILES - 1, COL_TILES - 1, 1], jnp.int32), SLOTS)
    return jnp.clip(index, 0, limit[None, :])


def body(features, weight, cotangent, tile_values, tile_rows, tile_cols, tile_valid):
    place = jnp.stack([lax.axis_index("core"), lax.axis_index("x")]).astype(jnp.int32)

    chunks = pl.pallas_call(
        spread,
        in_specs=[vmem()],
        out_specs=vmem(),
        out_shape=jax.ShapeDtypeStruct((COL_TILES, TILE, CHUNK), BF16),
        compiler_params=params(),
        name="spread",
    )(features)
    panel = lax.all_to_all(chunks, ("y", "x"), 0, 0, tiled=True)

    index = jnp.concatenate(
        [tile_rows.reshape(-1), tile_cols.reshape(-1), tile_valid.reshape(-1)]
    ).astype(BF16)
    index = jnp.pad(index[None, :], ((0, INDEX_ROWS - 1), (0, TILE - 3 * SLOTS)))
    tiles = jnp.concatenate([tile_values.reshape(SLOTS * TILE, TILE), index], axis=0)
    tiles = [tiles] + [exchange(tiles, "x", distance) for distance in range(1, X)]
    index = slots_of(tiles)

    mine, other = pl.pallas_call(
        forward_tiles,
        in_specs=[smem(), smem()] + [vmem()] * (1 + X),
        out_specs=[vmem()] * 2,
        out_shape=[jax.ShapeDtypeStruct((X * Z, TILE, CHUNK), BF16)] * 2,
        scratch_shapes=[pltpu.VMEM((ROW_TILES, TILE, CHUNK), F32)],
        compiler_params=params(),
        name="forward_tiles",
    )(place, index, panel, *tiles)
    term = (mine.astype(F32) + exchange(other, "core", 1).astype(F32)).astype(BF16)
    term, *theirs = lax.optimization_barrier((term, *tiles))
    parts = lax.all_to_all(term, ("x", "z"), 0, 0, tiled=True)
    theirs = [exchange(t, "core", 1) for t in theirs]
    all_index = jnp.concatenate([index, slots_of(theirs)])
    parts, all_index, *theirs = lax.optimization_barrier((parts, all_index, *theirs))

    half = WIDTH // CORES
    activations, grad, weight_keep, weight_send = pl.pallas_call(
        middle,
        in_specs=[smem()] + [vmem()] * 3,
        out_specs=[vmem()] * 4,
        out_shape=[
            jax.ShapeDtypeStruct((TILE, WIDTH), BF16),
            jax.ShapeDtypeStruct((X * ROW_TILES, TILE // 2, CHUNK), BF16),
            jax.ShapeDtypeStruct((half, WIDTH), BF16),
            jax.ShapeDtypeStruct((half, WIDTH), BF16),
        ],
        compiler_params=params(),
        name="middle",
    )(place, parts, weight, cotangent)

    panel = lax.all_to_all(grad, ("x", "z", "core"), 0, 0, tiled=True)
    piece = weight_keep.astype(F32) + exchange(weight_send, "core", 1).astype(F32)
    piece = piece.astype(BF16)
    for distance in (1, 2, 4):
        piece = halve(piece, "y", distance)
    panel, piece = lax.optimization_barrier((panel, piece))

    piece = double(piece, "z", 1)
    back = pl.pallas_call(
        backward_tiles,
        in_specs=[smem(), smem()] + [vmem()] * (1 + CORES * X),
        out_specs=vmem(),
        out_shape=jax.ShapeDtypeStruct((COL_TILES * CORES, TILE // 2, CHUNK), BF16),
        scratch_shapes=[
            pltpu.VMEM((X * ROW_TILES, TILE, CHUNK), BF16),
            pltpu.VMEM((COL_TILES, TILE, CHUNK), F32),
        ],
        compiler_params=params(),
        name="backward_tiles",
    )(place, all_index, panel, *tiles, *theirs)
    back, piece = lax.optimization_barrier((back, piece))
    back = lax.all_to_all(back, ("y", "x", "core"), 0, 0, tiled=True)
    for distance in (2, 4):
        piece = double(piece, "z", distance)
    piece = lax.all_gather(piece, "x", axis=0).astype(F32).sum(0).astype(BF16)
    back, piece = lax.optimization_barrier((back, piece))

    input_grad = pl.pallas_call(
        last,
        in_specs=[vmem()] * 2,
        out_specs=vmem(),
        out_shape=jax.ShapeDtypeStruct((TILE, WIDTH), BF16),
        compiler_params=params(),
        name="last",
    )(back, weight)

    share = WIDTH // (Y * CORES)
    piece = jnp.broadcast_to(piece[None], (Y, share, WIDTH))
    whole = lax.all_to_all(piece, "y", 0, 0, tiled=True)
    weight_grad = pl.pallas_call(
        place_rows,
        in_specs=[smem()] + [vmem()] * 2,
        out_specs=vmem(),
        out_shape=jax.ShapeDtypeStruct((WIDTH, WIDTH), F32),
        compiler_params=params(),
        name="place_rows",
    )(place, whole, exchange(whole, "core", 1))
    return (activations, input_grad, weight_grad)


def solution(mesh):
    axes = Mesh(mesh.devices.reshape(Y, X, Z, CORES), ("y", "x", "z", "core"))
    row, col = ("y", "x"), ("z", "core")
    placed = (
        P(col + row, None),
        P(),
        P(row + col, None),
        P(row, col, None, None, None),
        P(row, col, None),
        P(row, col, None),
        P(row, col, None),
    )
    return jax.shard_map(
        body,
        mesh=axes,
        in_specs=placed,
        out_specs=(P(row + col, None), P(col + row, None), P()),
        check_vma=False,
    )
```

```python
import math

import jax
import jax.numpy as jnp
from jax import lax
from jax.experimental import pallas as pl
from jax.experimental.pallas import tpu as pltpu
from jax.sharding import Mesh, PartitionSpec as P

Y, X, Z, CORES = 8, 4, 8, 2
TILE = 128
SLOTS = 8
WIDTH = 512
CHUNK = WIDTH // X
ROW_TILES = Z * CORES
COL_TILES = Y * X
INDEX_ROWS = 16
BF16 = jnp.bfloat16
F32 = jnp.float32


def params():
    return pltpu.CompilerParams(vmem_limit_bytes=24 * 1024 * 1024)


def vmem():
    return pl.BlockSpec(memory_space=pltpu.VMEM)


def smem():
    return pl.BlockSpec(memory_space=pltpu.SMEM)


def spread(features_ref, out_ref):
    for chunk in range(X):
        piece = features_ref[:, chunk * CHUNK : (chunk + 1) * CHUNK]
        for y in range(Y):
            out_ref[y * X + chunk] = piece


def forward_tiles(place_ref, index_ref, panel_ref, *refs):
    tiles_refs, (mine_ref, other_ref, total) = refs[:X], refs[X:]
    core = place_ref[0]
    for step in range(X):
        block = place_ref[1] ^ step
        total[...] = jnp.zeros_like(total)
        for slot in range(SLOTS):
            row = index_ref[step, slot]
            col = index_ref[step, SLOTS + slot]
            valid = index_ref[step, 2 * SLOTS + slot]
            tile = tiles_refs[step][slot * TILE : (slot + 1) * TILE, :]
            product = jnp.dot(tile, panel_ref[col], preferred_element_type=F32)
            total[row] += jnp.where(valid > 0, product, 0.0)
        for pair in range(Z):
            mine_ref[block * Z + pair] = total[2 * pair + core].astype(BF16)
            other_ref[block * Z + pair] = total[2 * pair + 1 - core].astype(BF16)


def middle(core_ref, parts_ref, weight_ref, cotangent_ref, act_ref, grad_ref, keep_ref, send_ref):
    chunks = []
    for chunk in range(X):
        total = parts_ref[chunk * Z].astype(F32)
        for z in range(1, Z):
            total += parts_ref[chunk * Z + z].astype(F32)
        chunks.append(total)
    summed = jnp.concatenate(chunks, axis=1)
    high = summed.astype(BF16)
    low = (summed - high.astype(F32)).astype(BF16)
    weight = weight_ref[...]
    aggregated = jnp.dot(high, weight, preferred_element_type=F32) + jnp.dot(
        low, weight, preferred_element_type=F32
    )
    sig = jax.nn.sigmoid(aggregated)
    act_ref[...] = (aggregated * sig).astype(BF16)
    grad = (cotangent_ref[...].astype(F32) * sig * (1.0 + aggregated * (1.0 - sig))).astype(BF16)
    for chunk in range(X):
        piece = grad[:, chunk * CHUNK : (chunk + 1) * CHUNK]
        for z in range(Z):
            grad_ref[chunk * Z + z] = piece
    weight_part = lax.dot_general(
        high, grad, (((0,), (0,)), ((), ())), preferred_element_type=F32
    ).astype(BF16)
    low_half, high_half = weight_part[: WIDTH // 2], weight_part[WIDTH // 2 :]
    upper = core_ref[0] == 1
    keep_ref[...] = jnp.where(upper, high_half, low_half)
    send_ref[...] = jnp.where(upper, low_half, high_half)


def backward_tiles(place_ref, index_ref, mine_ref, other_ref, *refs):
    tiles_refs, (out_ref, total) = refs[:X], refs[X:]
    core = place_ref[0]
    total[...] = jnp.zeros_like(total)
    for step in range(X):
        block = place_ref[1] ^ step
        for slot in range(SLOTS):
            row = index_ref[step, slot]
            col = index_ref[step, SLOTS + slot]
            valid = index_ref[step, 2 * SLOTS + slot]
            at = block * Z + row // 2
            panel = jnp.where(row % 2 == core, mine_ref[at], other_ref[at])
            tile = tiles_refs[step][slot * TILE : (slot + 1) * TILE, :]
            product = lax.dot_general(
                tile, panel, (((0,), (0,)), ((), ())), preferred_element_type=F32
            )
            total[col] += jnp.where(valid > 0, product, 0.0)
    for tile in range(COL_TILES):
        out_ref[tile] = total[tile].astype(BF16)


def last(parts_ref, weight_ref, out_ref):
    chunks = []
    for chunk in range(X):
        total = parts_ref[chunk].astype(F32)
        for y in range(1, Y):
            total += parts_ref[y * X + chunk].astype(F32)
        chunks.append(total)
    summed = jnp.concatenate(chunks, axis=1).astype(BF16)
    out_ref[...] = lax.dot_general(
        summed, weight_ref[...], (((1,), (1,)), ((), ())), preferred_element_type=F32
    ).astype(BF16)


def place_rows(place_ref, mine_ref, other_ref, out_ref):
    core = place_ref[0]
    half, share = WIDTH // CORES, WIDTH // (X * CORES)
    scale = 1.0 / math.sqrt(TILE * Y * X * Z * CORES)
    for x in range(X):
        at = ((x & 1) * 2 + (x >> 1)) * share
        for side, ref in ((core, mine_ref), (1 - core, other_ref)):
            start = pl.multiple_of(side * half + at, share)
            out_ref[pl.ds(start, share), :] = ref[x].astype(F32) * scale


def exchange(array, axis, distance):
    size = lax.axis_size(axis)
    return lax.ppermute(array, axis, [(i, i ^ distance) for i in range(size)])


def halve(array, axis, distance):
    upper = jnp.minimum(lax.axis_index(axis) & distance, 1)
    halves = array.reshape(2, array.shape[0] // 2, array.shape[1])
    send = lax.dynamic_index_in_dim(halves, 1 - upper, 0, keepdims=False)
    keep = lax.dynamic_index_in_dim(halves, upper, 0, keepdims=False)
    return (keep.astype(F32) + exchange(send, axis, distance).astype(F32)).astype(BF16)


def double(array, axis, distance):
    return (array.astype(F32) + exchange(array, axis, distance).astype(F32)).astype(BF16)


def body(features, weight, cotangent, tile_values, tile_rows, tile_cols, tile_valid):
    place = jnp.stack([lax.axis_index("core"), lax.axis_index("x")]).astype(jnp.int32)

    chunks = pl.pallas_call(
        spread,
        in_specs=[vmem()],
        out_specs=vmem(),
        out_shape=jax.ShapeDtypeStruct((COL_TILES, TILE, CHUNK), BF16),
        compiler_params=params(),
        name="spread",
    )(features)
    panel = lax.all_to_all(chunks, ("y", "x"), 0, 0, tiled=True)

    index = jnp.concatenate(
        [tile_rows.reshape(-1), tile_cols.reshape(-1), tile_valid.reshape(-1)]
    ).astype(BF16)
    index = jnp.pad(index[None, :], ((0, INDEX_ROWS - 1), (0, TILE - 3 * SLOTS)))
    tiles = jnp.concatenate([tile_values.reshape(SLOTS * TILE, TILE), index], axis=0)
    tiles = [tiles] + [exchange(tiles, "x", distance) for distance in range(1, X)]
    index = jnp.stack([t[SLOTS * TILE, : 3 * SLOTS] for t in tiles]).astype(jnp.int32)
    limit = jnp.repeat(jnp.array([ROW_TILES - 1, COL_TILES - 1, 1], jnp.int32), SLOTS)
    index = jnp.clip(index, 0, limit[None, :])

    mine, other = pl.pallas_call(
        forward_tiles,
        in_specs=[smem(), smem()] + [vmem()] * (1 + X),
        out_specs=[vmem()] * 2,
        out_shape=[jax.ShapeDtypeStruct((X * Z, TILE, CHUNK), BF16)] * 2,
        scratch_shapes=[pltpu.VMEM((ROW_TILES, TILE, CHUNK), F32)],
        compiler_params=params(),
        name="forward_tiles",
    )(place, index, panel, *tiles)
    term = (mine.astype(F32) + exchange(other, "core", 1).astype(F32)).astype(BF16)
    parts = lax.all_to_all(term, ("x", "z"), 0, 0, tiled=True)

    half = WIDTH // CORES
    activations, grad, weight_keep, weight_send = pl.pallas_call(
        middle,
        in_specs=[smem()] + [vmem()] * 3,
        out_specs=[vmem()] * 4,
        out_shape=[
            jax.ShapeDtypeStruct((TILE, WIDTH), BF16),
            jax.ShapeDtypeStruct((X * Z, TILE, CHUNK), BF16),
            jax.ShapeDtypeStruct((half, WIDTH), BF16),
            jax.ShapeDtypeStruct((half, WIDTH), BF16),
        ],
        compiler_params=params(),
        name="middle",
    )(place, parts, weight, cotangent)

    grad_mine = lax.all_to_all(grad, ("x", "z"), 0, 0, tiled=True)
    piece = weight_keep.astype(F32) + exchange(weight_send, "core", 1).astype(F32)
    piece = piece.astype(BF16)
    for distance in (1, 2):
        piece = halve(piece, "x", distance)
    piece = double(piece, "y", 1)
    grad_mine, piece = lax.optimization_barrier((grad_mine, piece))

    grad_other = exchange(grad_mine, "core", 1)
    piece = double(piece, "z", 1)
    back = pl.pallas_call(
        backward_tiles,
        in_specs=[smem(), smem()] + [vmem()] * (2 + X),
        out_specs=vmem(),
        out_shape=jax.ShapeDtypeStruct((COL_TILES, TILE, CHUNK), BF16),
        scratch_shapes=[pltpu.VMEM((COL_TILES, TILE, CHUNK), F32)],
        compiler_params=params(),
        name="backward_tiles",
    )(place, index, grad_mine, grad_other, *tiles)
    back, piece = lax.optimization_barrier((back, piece))
    back = lax.all_to_all(back, ("y", "x"), 0, 0, tiled=True)
    for axis, distance in (("y", 2), ("y", 4), ("z", 2), ("z", 4)):
        piece = double(piece, axis, distance)
    back, piece = lax.optimization_barrier((back, piece))

    input_grad = pl.pallas_call(
        last,
        in_specs=[vmem()] * 2,
        out_specs=vmem(),
        out_shape=jax.ShapeDtypeStruct((TILE, WIDTH), BF16),
        compiler_params=params(),
        name="last",
    )(back, weight)

    share = WIDTH // (X * CORES)
    piece = jnp.broadcast_to(piece[None], (X, share, WIDTH))
    whole = lax.all_to_all(piece, "x", 0, 0, tiled=True)
    weight_grad = pl.pallas_call(
        place_rows,
        in_specs=[smem()] + [vmem()] * 2,
        out_specs=vmem(),
        out_shape=jax.ShapeDtypeStruct((WIDTH, WIDTH), F32),
        compiler_params=params(),
        name="place_rows",
    )(place, whole, exchange(whole, "core", 1))
    return (activations, input_grad, weight_grad)


def solution(mesh):
    axes = Mesh(mesh.devices.reshape(Y, X, Z, CORES), ("y", "x", "z", "core"))
    row, col = ("y", "x"), ("z", "core")
    placed = (
        P(col + row, None),
        P(),
        P(row + col, None),
        P(row, col, None, None, None),
        P(row, col, None),
        P(row, col, None),
        P(row, col, None),
    )
    return jax.shard_map(
        body,
        mesh=axes,
        in_specs=placed,
        out_specs=(P(row + col, None), P(col + row, None), P()),
        check_vma=False,
    )
```

```python
import math

import jax
import jax.numpy as jnp
from jax import lax
from jax.experimental import pallas as pl
from jax.experimental.pallas import tpu as pltpu
from jax.sharding import Mesh, PartitionSpec as P

Y, X, Z, CORES = 8, 4, 8, 2
TILE = 128
SLOTS = 8
WIDTH = 512
CHUNK = WIDTH // X
ROW_TILES = Z * CORES
COL_TILES = Y * X
INDEX_ROWS = 16
BF16 = jnp.bfloat16
F32 = jnp.float32


def params():
    return pltpu.CompilerParams(vmem_limit_bytes=24 * 1024 * 1024)


def vmem():
    return pl.BlockSpec(memory_space=pltpu.VMEM)


def smem():
    return pl.BlockSpec(memory_space=pltpu.SMEM)


def spread(features_ref, out_ref):
    for chunk in range(X):
        piece = features_ref[:, chunk * CHUNK : (chunk + 1) * CHUNK]
        for y in range(Y):
            out_ref[y * X + chunk] = piece


def forward_tiles(place_ref, index_ref, panel_ref, *refs):
    tiles_refs, (mine_ref, other_ref, total) = refs[:X], refs[X:]
    core = place_ref[0]
    for step in range(X):
        block = place_ref[1] ^ step
        total[...] = jnp.zeros_like(total)
        for slot in range(SLOTS):
            row = index_ref[step, slot]
            col = index_ref[step, SLOTS + slot]
            valid = index_ref[step, 2 * SLOTS + slot]
            tile = tiles_refs[step][slot * TILE : (slot + 1) * TILE, :]
            product = jnp.dot(tile, panel_ref[col], preferred_element_type=F32)
            total[row] += jnp.where(valid > 0, product, 0.0)
        for pair in range(Z):
            mine_ref[block * Z + pair] = total[2 * pair + core].astype(BF16)
            other_ref[block * Z + pair] = total[2 * pair + 1 - core].astype(BF16)


def middle(core_ref, parts_ref, weight_ref, cotangent_ref, act_ref, grad_ref, keep_ref, send_ref):
    chunks = []
    for chunk in range(X):
        total = parts_ref[chunk * Z].astype(F32)
        for z in range(1, Z):
            total += parts_ref[chunk * Z + z].astype(F32)
        chunks.append(total)
    summed = jnp.concatenate(chunks, axis=1)
    high = summed.astype(BF16)
    low = (summed - high.astype(F32)).astype(BF16)
    weight = weight_ref[...]
    aggregated = jnp.dot(high, weight, preferred_element_type=F32) + jnp.dot(
        low, weight, preferred_element_type=F32
    )
    sig = jax.nn.sigmoid(aggregated)
    act_ref[...] = (aggregated * sig).astype(BF16)
    grad = (cotangent_ref[...].astype(F32) * sig * (1.0 + aggregated * (1.0 - sig))).astype(BF16)
    for chunk in range(X):
        piece = grad[:, chunk * CHUNK : (chunk + 1) * CHUNK]
        for z in range(Z):
            grad_ref[chunk * Z + z] = piece
    weight_part = lax.dot_general(
        high, grad, (((0,), (0,)), ((), ())), preferred_element_type=F32
    ).astype(BF16)
    low_half, high_half = weight_part[: WIDTH // 2], weight_part[WIDTH // 2 :]
    upper = core_ref[0] == 1
    keep_ref[...] = jnp.where(upper, high_half, low_half)
    send_ref[...] = jnp.where(upper, low_half, high_half)


def backward_tiles(place_ref, index_ref, mine_ref, other_ref, *refs):
    tiles_refs, (out_ref, total) = refs[:X], refs[X:]
    core = place_ref[0]
    total[...] = jnp.zeros_like(total)
    for step in range(X):
        block = place_ref[1] ^ step
        for slot in range(SLOTS):
            row = index_ref[step, slot]
            col = index_ref[step, SLOTS + slot]
            valid = index_ref[step, 2 * SLOTS + slot]
            at = block * Z + row // 2
            panel = jnp.where(row % 2 == core, mine_ref[at], other_ref[at])
            tile = tiles_refs[step][slot * TILE : (slot + 1) * TILE, :]
            product = lax.dot_general(
                tile, panel, (((0,), (0,)), ((), ())), preferred_element_type=F32
            )
            total[col] += jnp.where(valid > 0, product, 0.0)
    for tile in range(COL_TILES):
        out_ref[tile] = total[tile].astype(BF16)


def last(parts_ref, weight_ref, out_ref):
    chunks = []
    for chunk in range(X):
        total = parts_ref[chunk].astype(F32)
        for y in range(1, Y):
            total += parts_ref[y * X + chunk].astype(F32)
        chunks.append(total)
    summed = jnp.concatenate(chunks, axis=1).astype(BF16)
    out_ref[...] = lax.dot_general(
        summed, weight_ref[...], (((1,), (1,)), ((), ())), preferred_element_type=F32
    ).astype(BF16)


def place_rows(place_ref, mine_ref, other_ref, out_ref):
    core = place_ref[0]
    half, share = WIDTH // CORES, WIDTH // (X * CORES)
    scale = 1.0 / math.sqrt(TILE * Y * X * Z * CORES)
    for x in range(X):
        for side, ref in ((core, mine_ref), (1 - core, other_ref)):
            start = pl.multiple_of(side * half + x * share, share)
            out_ref[pl.ds(start, share), :] = ref[x].astype(F32) * scale


def exchange(array, axis, distance):
    size = lax.axis_size(axis)
    return lax.ppermute(array, axis, [(i, i ^ distance) for i in range(size)])


def scatter(array, axis):
    size, place = lax.axis_size(axis), lax.axis_index(axis)
    shares = array.reshape(size, array.shape[0] // size, array.shape[1])

    def share(distance):
        return lax.dynamic_index_in_dim(shares, place ^ distance, 0, keepdims=False)

    total = share(0).astype(F32)
    for distance in range(1, size):
        total = total + exchange(share(distance), axis, distance).astype(F32)
    return total.astype(BF16)


def double(array, axis, distance):
    return (array.astype(F32) + exchange(array, axis, distance).astype(F32)).astype(BF16)


def body(features, weight, cotangent, tile_values, tile_rows, tile_cols, tile_valid):
    place = jnp.stack([lax.axis_index("core"), lax.axis_index("x")]).astype(jnp.int32)

    chunks = pl.pallas_call(
        spread,
        in_specs=[vmem()],
        out_specs=vmem(),
        out_shape=jax.ShapeDtypeStruct((COL_TILES, TILE, CHUNK), BF16),
        compiler_params=params(),
        name="spread",
    )(features)
    panel = lax.all_to_all(chunks, ("y", "x"), 0, 0, tiled=True)

    index = jnp.concatenate(
        [tile_rows.reshape(-1), tile_cols.reshape(-1), tile_valid.reshape(-1)]
    ).astype(BF16)
    index = jnp.pad(index[None, :], ((0, INDEX_ROWS - 1), (0, TILE - 3 * SLOTS)))
    tiles = jnp.concatenate([tile_values.reshape(SLOTS * TILE, TILE), index], axis=0)
    tiles = [tiles] + [exchange(tiles, "x", distance) for distance in range(1, X)]
    index = jnp.stack([t[SLOTS * TILE, : 3 * SLOTS] for t in tiles]).astype(jnp.int32)
    limit = jnp.repeat(jnp.array([ROW_TILES - 1, COL_TILES - 1, 1], jnp.int32), SLOTS)
    index = jnp.clip(index, 0, limit[None, :])

    mine, other = pl.pallas_call(
        forward_tiles,
        in_specs=[smem(), smem()] + [vmem()] * (1 + X),
        out_specs=[vmem()] * 2,
        out_shape=[jax.ShapeDtypeStruct((X * Z, TILE, CHUNK), BF16)] * 2,
        scratch_shapes=[pltpu.VMEM((ROW_TILES, TILE, CHUNK), F32)],
        compiler_params=params(),
        name="forward_tiles",
    )(place, index, panel, *tiles)
    term = (mine.astype(F32) + exchange(other, "core", 1).astype(F32)).astype(BF16)
    parts = lax.all_to_all(term, ("x", "z"), 0, 0, tiled=True)

    half = WIDTH // CORES
    activations, grad, weight_keep, weight_send = pl.pallas_call(
        middle,
        in_specs=[smem()] + [vmem()] * 3,
        out_specs=[vmem()] * 4,
        out_shape=[
            jax.ShapeDtypeStruct((TILE, WIDTH), BF16),
            jax.ShapeDtypeStruct((X * Z, TILE, CHUNK), BF16),
            jax.ShapeDtypeStruct((half, WIDTH), BF16),
            jax.ShapeDtypeStruct((half, WIDTH), BF16),
        ],
        compiler_params=params(),
        name="middle",
    )(place, parts, weight, cotangent)

    grad_mine = lax.all_to_all(grad, ("x", "z"), 0, 0, tiled=True)
    piece = weight_keep.astype(F32) + exchange(weight_send, "core", 1).astype(F32)
    piece = piece.astype(BF16)
    piece = scatter(piece, "x")
    for distance in (1, 2):
        piece = double(piece, "y", distance)
    grad_mine, piece = lax.optimization_barrier((grad_mine, piece))

    grad_other = exchange(grad_mine, "core", 1)
    piece = double(piece, "y", 4)
    back = pl.pallas_call(
        backward_tiles,
        in_specs=[smem(), smem()] + [vmem()] * (2 + X),
        out_specs=vmem(),
        out_shape=jax.ShapeDtypeStruct((COL_TILES, TILE, CHUNK), BF16),
        scratch_shapes=[pltpu.VMEM((COL_TILES, TILE, CHUNK), F32)],
        compiler_params=params(),
        name="backward_tiles",
    )(place, index, grad_mine, grad_other, *tiles)
    back, piece = lax.optimization_barrier((back, piece))
    back = lax.all_to_all(back, ("y", "x"), 0, 0, tiled=True)
    for distance in (1, 2, 4):
        piece = double(piece, "z", distance)
    back, piece = lax.optimization_barrier((back, piece))

    input_grad = pl.pallas_call(
        last,
        in_specs=[vmem()] * 2,
        out_specs=vmem(),
        out_shape=jax.ShapeDtypeStruct((TILE, WIDTH), BF16),
        compiler_params=params(),
        name="last",
    )(back, weight)

    share = WIDTH // (X * CORES)
    piece = jnp.broadcast_to(piece[None], (X, share, WIDTH))
    whole = lax.all_to_all(piece, "x", 0, 0, tiled=True)
    weight_grad = pl.pallas_call(
        place_rows,
        in_specs=[smem()] + [vmem()] * 2,
        out_specs=vmem(),
        out_shape=jax.ShapeDtypeStruct((WIDTH, WIDTH), F32),
        compiler_params=params(),
        name="place_rows",
    )(place, whole, exchange(whole, "core", 1))
    return (activations, input_grad, weight_grad)


def solution(mesh):
    axes = Mesh(mesh.devices.reshape(Y, X, Z, CORES), ("y", "x", "z", "core"))
    row, col = ("y", "x"), ("z", "core")
    placed = (
        P(col + row, None),
        P(),
        P(row + col, None),
        P(row, col, None, None, None),
        P(row, col, None),
        P(row, col, None),
        P(row, col, None),
    )
    return jax.shard_map(
        body,
        mesh=axes,
        in_specs=placed,
        out_specs=(P(row + col, None), P(col + row, None), P()),
        check_vma=False,
    )
```

```python
import math

import jax
import jax.numpy as jnp
from jax import lax
from jax.experimental import pallas as pl
from jax.experimental.pallas import tpu as pltpu
from jax.sharding import Mesh, PartitionSpec as P

Y, X, Z, CORES = 8, 4, 8, 2
TILE = 128
SLOTS = 8
WIDTH = 512
CHUNK = WIDTH // X
ROW_TILES = Z * CORES
COL_TILES = Y * X
INDEX_ROWS = 16
BF16 = jnp.bfloat16
F32 = jnp.float32


def params():
    return pltpu.CompilerParams(vmem_limit_bytes=24 * 1024 * 1024)


def vmem():
    return pl.BlockSpec(memory_space=pltpu.VMEM)


def smem():
    return pl.BlockSpec(memory_space=pltpu.SMEM)


def spread(features_ref, out_ref):
    for chunk in range(X):
        piece = features_ref[:, chunk * CHUNK : (chunk + 1) * CHUNK]
        for y in range(Y):
            out_ref[y * X + chunk] = piece


def forward_tiles(place_ref, index_ref, panel_ref, *refs):
    tiles_refs, (mine_ref, other_ref, total) = refs[:X], refs[X:]
    core = place_ref[0]
    for step in range(X):
        block = place_ref[1] ^ step
        total[...] = jnp.zeros_like(total)
        for slot in range(SLOTS):
            row = index_ref[step, slot]
            col = index_ref[step, SLOTS + slot]
            valid = index_ref[step, 2 * SLOTS + slot]
            tile = tiles_refs[step][slot * TILE : (slot + 1) * TILE, :]
            product = jnp.dot(tile, panel_ref[col], preferred_element_type=F32)
            total[row] += jnp.where(valid > 0, product, 0.0)
        for pair in range(Z):
            mine_ref[block * Z + pair] = total[2 * pair + core].astype(BF16)
            other_ref[block * Z + pair] = total[2 * pair + 1 - core].astype(BF16)


def middle(core_ref, parts_ref, weight_ref, cotangent_ref, act_ref, grad_ref, keep_ref, send_ref):
    chunks = []
    for chunk in range(X):
        total = parts_ref[chunk * Z].astype(F32)
        for z in range(1, Z):
            total += parts_ref[chunk * Z + z].astype(F32)
        chunks.append(total)
    summed = jnp.concatenate(chunks, axis=1)
    high = summed.astype(BF16)
    low = (summed - high.astype(F32)).astype(BF16)
    weight = weight_ref[...]
    aggregated = jnp.dot(high, weight, preferred_element_type=F32) + jnp.dot(
        low, weight, preferred_element_type=F32
    )
    sig = jax.nn.sigmoid(aggregated)
    act_ref[...] = (aggregated * sig).astype(BF16)
    grad = (cotangent_ref[...].astype(F32) * sig * (1.0 + aggregated * (1.0 - sig))).astype(BF16)
    for chunk in range(X):
        piece = grad[:, chunk * CHUNK : (chunk + 1) * CHUNK]
        for z in range(Z):
            grad_ref[chunk * Z + z] = piece
    weight_part = lax.dot_general(
        high, grad, (((0,), (0,)), ((), ())), preferred_element_type=F32
    ).astype(BF16)
    low_half, high_half = weight_part[: WIDTH // 2], weight_part[WIDTH // 2 :]
    upper = core_ref[0] == 1
    keep_ref[...] = jnp.where(upper, high_half, low_half)
    send_ref[...] = jnp.where(upper, low_half, high_half)


def backward_tiles(place_ref, index_ref, mine_ref, other_ref, *refs):
    tiles_refs, (out_ref, total) = refs[:X], refs[X:]
    core = place_ref[0]
    total[...] = jnp.zeros_like(total)
    for step in range(X):
        block = place_ref[1] ^ step
        for slot in range(SLOTS):
            row = index_ref[step, slot]
            col = index_ref[step, SLOTS + slot]
            valid = index_ref[step, 2 * SLOTS + slot]
            at = block * Z + row // 2
            panel = jnp.where(row % 2 == core, mine_ref[at], other_ref[at])
            tile = tiles_refs[step][slot * TILE : (slot + 1) * TILE, :]
            product = lax.dot_general(
                tile, panel, (((0,), (0,)), ((), ())), preferred_element_type=F32
            )
            total[col] += jnp.where(valid > 0, product, 0.0)
    for tile in range(COL_TILES):
        out_ref[tile] = total[tile].astype(BF16)


def last(parts_ref, weight_ref, out_ref):
    chunks = []
    for chunk in range(X):
        total = parts_ref[chunk].astype(F32)
        for y in range(1, Y):
            total += parts_ref[y * X + chunk].astype(F32)
        chunks.append(total)
    summed = jnp.concatenate(chunks, axis=1).astype(BF16)
    out_ref[...] = lax.dot_general(
        summed, weight_ref[...], (((1,), (1,)), ((), ())), preferred_element_type=F32
    ).astype(BF16)


def place_rows(place_ref, mine_ref, other_ref, out_ref):
    core = place_ref[0]
    half, share = WIDTH // CORES, WIDTH // (X * CORES)
    scale = 1.0 / math.sqrt(TILE * Y * X * Z * CORES)
    for x in range(X):
        for side, ref in ((core, mine_ref), (1 - core, other_ref)):
            start = pl.multiple_of(side * half + x * share, share)
            out_ref[pl.ds(start, share), :] = ref[x].astype(F32) * scale


def exchange(array, axis, distance):
    size = lax.axis_size(axis)
    return lax.ppermute(array, axis, [(i, i ^ distance) for i in range(size)])


def scatter(array, axis):
    size, place = lax.axis_size(axis), lax.axis_index(axis)
    shares = array.reshape(size, array.shape[0] // size, array.shape[1])

    def share(distance):
        return lax.dynamic_index_in_dim(shares, place ^ distance, 0, keepdims=False)

    total = share(0).astype(F32)
    for distance in range(1, size):
        total = total + exchange(share(distance), axis, distance).astype(F32)
    return total.astype(BF16)


def double(array, axis, distance):
    return (array.astype(F32) + exchange(array, axis, distance).astype(F32)).astype(BF16)


def double4(array, axis):
    one, two, three = (exchange(array, axis, distance).astype(F32) for distance in (1, 2, 3))
    return ((array.astype(F32) + one) + (two + three)).astype(BF16)


def body(features, weight, cotangent, tile_values, tile_rows, tile_cols, tile_valid):
    place = jnp.stack([lax.axis_index("core"), lax.axis_index("x")]).astype(jnp.int32)

    chunks = pl.pallas_call(
        spread,
        in_specs=[vmem()],
        out_specs=vmem(),
        out_shape=jax.ShapeDtypeStruct((COL_TILES, TILE, CHUNK), BF16),
        compiler_params=params(),
        name="spread",
    )(features)
    panel = lax.all_to_all(chunks, ("y", "x"), 0, 0, tiled=True)

    index = jnp.concatenate(
        [tile_rows.reshape(-1), tile_cols.reshape(-1), tile_valid.reshape(-1)]
    ).astype(BF16)
    index = jnp.pad(index[None, :], ((0, INDEX_ROWS - 1), (0, TILE - 3 * SLOTS)))
    tiles = jnp.concatenate([tile_values.reshape(SLOTS * TILE, TILE), index], axis=0)
    tiles = [tiles] + [exchange(tiles, "x", distance) for distance in range(1, X)]
    index = jnp.stack([t[SLOTS * TILE, : 3 * SLOTS] for t in tiles]).astype(jnp.int32)
    limit = jnp.repeat(jnp.array([ROW_TILES - 1, COL_TILES - 1, 1], jnp.int32), SLOTS)
    index = jnp.clip(index, 0, limit[None, :])

    mine, other = pl.pallas_call(
        forward_tiles,
        in_specs=[smem(), smem()] + [vmem()] * (1 + X),
        out_specs=[vmem()] * 2,
        out_shape=[jax.ShapeDtypeStruct((X * Z, TILE, CHUNK), BF16)] * 2,
        scratch_shapes=[pltpu.VMEM((ROW_TILES, TILE, CHUNK), F32)],
        compiler_params=params(),
        name="forward_tiles",
    )(place, index, panel, *tiles)
    term = (mine.astype(F32) + exchange(other, "core", 1).astype(F32)).astype(BF16)
    parts = lax.all_to_all(term, ("x", "z"), 0, 0, tiled=True)

    half = WIDTH // CORES
    activations, grad, weight_keep, weight_send = pl.pallas_call(
        middle,
        in_specs=[smem()] + [vmem()] * 3,
        out_specs=[vmem()] * 4,
        out_shape=[
            jax.ShapeDtypeStruct((TILE, WIDTH), BF16),
            jax.ShapeDtypeStruct((X * Z, TILE, CHUNK), BF16),
            jax.ShapeDtypeStruct((half, WIDTH), BF16),
            jax.ShapeDtypeStruct((half, WIDTH), BF16),
        ],
        compiler_params=params(),
        name="middle",
    )(place, parts, weight, cotangent)

    grad_mine = lax.all_to_all(grad, ("x", "z"), 0, 0, tiled=True)
    piece = weight_keep.astype(F32) + exchange(weight_send, "core", 1).astype(F32)
    piece = piece.astype(BF16)
    piece = scatter(piece, "x")
    piece = double4(piece, "y")
    grad_mine, piece = lax.optimization_barrier((grad_mine, piece))

    grad_other = exchange(grad_mine, "core", 1)
    piece = double(piece, "y", Y - 1)
    back = pl.pallas_call(
        backward_tiles,
        in_specs=[smem(), smem()] + [vmem()] * (2 + X),
        out_specs=vmem(),
        out_shape=jax.ShapeDtypeStruct((COL_TILES, TILE, CHUNK), BF16),
        scratch_shapes=[pltpu.VMEM((COL_TILES, TILE, CHUNK), F32)],
        compiler_params=params(),
        name="backward_tiles",
    )(place, index, grad_mine, grad_other, *tiles)
    back, piece = lax.optimization_barrier((back, piece))
    back = lax.all_to_all(back, ("y", "x"), 0, 0, tiled=True)
    for distance in (1, 2, Z - 1):
        piece = double(piece, "z", distance)
    back, piece = lax.optimization_barrier((back, piece))

    input_grad = pl.pallas_call(
        last,
        in_specs=[vmem()] * 2,
        out_specs=vmem(),
        out_shape=jax.ShapeDtypeStruct((TILE, WIDTH), BF16),
        compiler_params=params(),
        name="last",
    )(back, weight)

    share = WIDTH // (X * CORES)
    piece = jnp.broadcast_to(piece[None], (X, share, WIDTH))
    whole = lax.all_to_all(piece, "x", 0, 0, tiled=True)
    weight_grad = pl.pallas_call(
        place_rows,
        in_specs=[smem()] + [vmem()] * 2,
        out_specs=vmem(),
        out_shape=jax.ShapeDtypeStruct((WIDTH, WIDTH), F32),
        compiler_params=params(),
        name="place_rows",
    )(place, whole, exchange(whole, "core", 1))
    return (activations, input_grad, weight_grad)


def solution(mesh):
    axes = Mesh(mesh.devices.reshape(Y, X, Z, CORES), ("y", "x", "z", "core"))
    row, col = ("y", "x"), ("z", "core")
    placed = (
        P(col + row, None),
        P(),
        P(row + col, None),
        P(row, col, None, None, None),
        P(row, col, None),
        P(row, col, None),
        P(row, col, None),
    )
    return jax.shard_map(
        body,
        mesh=axes,
        in_specs=placed,
        out_specs=(P(row + col, None), P(col + row, None), P()),
        check_vma=False,
    )
```

```python
import math

import jax
import jax.numpy as jnp
from jax import lax
from jax.experimental import pallas as pl
from jax.experimental.pallas import tpu as pltpu
from jax.sharding import Mesh, PartitionSpec as P

Y, X, Z, CORES = 8, 4, 8, 2
TILE = 128
SLOTS = 8
WIDTH = 512
CHUNK = WIDTH // X
ROW_TILES = Z * CORES
COL_TILES = Y * X
INDEX_ROWS = 16
BF16 = jnp.bfloat16
F32 = jnp.float32


def params():
    return pltpu.CompilerParams(vmem_limit_bytes=24 * 1024 * 1024)


def vmem():
    return pl.BlockSpec(memory_space=pltpu.VMEM)


def smem():
    return pl.BlockSpec(memory_space=pltpu.SMEM)


def spread(features_ref, out_ref):
    for chunk in range(X):
        piece = features_ref[:, chunk * CHUNK : (chunk + 1) * CHUNK]
        for y in range(Y):
            out_ref[y * X + chunk] = piece


def forward_tiles(place_ref, index_ref, panel_ref, *refs):
    tiles_refs, (mine_ref, other_ref, total) = refs[:X], refs[X:]
    core = place_ref[0]
    for step in range(X):
        block = place_ref[1] ^ step
        total[...] = jnp.zeros_like(total)
        for slot in range(SLOTS):
            row = index_ref[step, slot]
            col = index_ref[step, SLOTS + slot]
            valid = index_ref[step, 2 * SLOTS + slot]
            tile = tiles_refs[step][slot * TILE : (slot + 1) * TILE, :]
            product = jnp.dot(tile, panel_ref[col], preferred_element_type=F32)
            total[row] += jnp.where(valid > 0, product, 0.0)
        for pair in range(Z):
            mine_ref[block * Z + pair] = total[2 * pair + core].astype(BF16)
            other_ref[block * Z + pair] = total[2 * pair + 1 - core].astype(BF16)


def middle(parts_ref, weight_ref, cotangent_ref, act_ref, grad_ref, weight_part_ref):
    chunks = []
    for chunk in range(X):
        total = parts_ref[chunk * Z].astype(F32)
        for z in range(1, Z):
            total += parts_ref[chunk * Z + z].astype(F32)
        chunks.append(total)
    summed = jnp.concatenate(chunks, axis=1)
    high = summed.astype(BF16)
    low = (summed - high.astype(F32)).astype(BF16)
    weight = weight_ref[...]
    aggregated = jnp.dot(high, weight, preferred_element_type=F32) + jnp.dot(
        low, weight, preferred_element_type=F32
    )
    sig = jax.nn.sigmoid(aggregated)
    act_ref[...] = (aggregated * sig).astype(BF16)
    grad = (cotangent_ref[...].astype(F32) * sig * (1.0 + aggregated * (1.0 - sig))).astype(BF16)
    for chunk in range(X):
        piece = grad[:, chunk * CHUNK : (chunk + 1) * CHUNK]
        for z in range(Z):
            grad_ref[chunk * Z + z] = piece
    weight_part_ref[...] = lax.dot_general(
        high, grad, (((0,), (0,)), ((), ())), preferred_element_type=F32
    ).astype(BF16)


def backward_tiles(place_ref, index_ref, mine_ref, other_ref, *refs):
    tiles_refs, (out_ref, total) = refs[:X], refs[X:]
    core = place_ref[0]
    total[...] = jnp.zeros_like(total)
    for step in range(X):
        block = place_ref[1] ^ step
        for slot in range(SLOTS):
            row = index_ref[step, slot]
            col = index_ref[step, SLOTS + slot]
            valid = index_ref[step, 2 * SLOTS + slot]
            at = block * Z + row // 2
            panel = jnp.where(row % 2 == core, mine_ref[at], other_ref[at])
            tile = tiles_refs[step][slot * TILE : (slot + 1) * TILE, :]
            product = lax.dot_general(
                tile, panel, (((0,), (0,)), ((), ())), preferred_element_type=F32
            )
            total[col] += jnp.where(valid > 0, product, 0.0)
    for tile in range(COL_TILES):
        out_ref[tile] = total[tile].astype(BF16)


def last(parts_ref, weight_ref, out_ref):
    chunks = []
    for chunk in range(X):
        total = parts_ref[chunk].astype(F32)
        for y in range(1, Y):
            total += parts_ref[y * X + chunk].astype(F32)
        chunks.append(total)
    summed = jnp.concatenate(chunks, axis=1).astype(BF16)
    out_ref[...] = lax.dot_general(
        summed, weight_ref[...], (((1,), (1,)), ((), ())), preferred_element_type=F32
    ).astype(BF16)


def exchange(array, axis, distance):
    size = lax.axis_size(axis)
    return lax.ppermute(array, axis, [(i, i ^ distance) for i in range(size)])


def scatter(array, axis):
    size, place = lax.axis_size(axis), lax.axis_index(axis)
    shares = array.reshape(size, array.shape[0] // size, array.shape[1])

    def share(distance):
        return lax.dynamic_index_in_dim(shares, place ^ distance, 0, keepdims=False)

    total = share(0).astype(F32)
    for distance in range(1, size):
        total = total + exchange(share(distance), axis, distance).astype(F32)
    return total.astype(BF16)


def double(array, axis, distance):
    return (array.astype(F32) + exchange(array, axis, distance).astype(F32)).astype(BF16)


def double4(array, axis):
    one, two, three = (exchange(array, axis, distance).astype(F32) for distance in (1, 2, 3))
    return ((array.astype(F32) + one) + (two + three)).astype(BF16)


def body(features, weight, cotangent, tile_values, tile_rows, tile_cols, tile_valid):
    place = jnp.stack([lax.axis_index("core"), lax.axis_index("x")]).astype(jnp.int32)

    chunks = pl.pallas_call(
        spread,
        in_specs=[vmem()],
        out_specs=vmem(),
        out_shape=jax.ShapeDtypeStruct((COL_TILES, TILE, CHUNK), BF16),
        compiler_params=params(),
        name="spread",
    )(features)
    panel = lax.all_to_all(chunks, ("y", "x"), 0, 0, tiled=True)

    index = jnp.concatenate(
        [tile_rows.reshape(-1), tile_cols.reshape(-1), tile_valid.reshape(-1)]
    ).astype(BF16)
    index = jnp.pad(index[None, :], ((0, INDEX_ROWS - 1), (0, TILE - 3 * SLOTS)))
    tiles = jnp.concatenate([tile_values.reshape(SLOTS * TILE, TILE), index], axis=0)
    tiles = [tiles] + [exchange(tiles, "x", distance) for distance in range(1, X)]
    index = jnp.stack([t[SLOTS * TILE, : 3 * SLOTS] for t in tiles]).astype(jnp.int32)
    limit = jnp.repeat(jnp.array([ROW_TILES - 1, COL_TILES - 1, 1], jnp.int32), SLOTS)
    index = jnp.clip(index, 0, limit[None, :])

    mine, other = pl.pallas_call(
        forward_tiles,
        in_specs=[smem(), smem()] + [vmem()] * (1 + X),
        out_specs=[vmem()] * 2,
        out_shape=[jax.ShapeDtypeStruct((X * Z, TILE, CHUNK), BF16)] * 2,
        scratch_shapes=[pltpu.VMEM((ROW_TILES, TILE, CHUNK), F32)],
        compiler_params=params(),
        name="forward_tiles",
    )(place, index, panel, *tiles)
    term = (mine.astype(F32) + exchange(other, "core", 1).astype(F32)).astype(BF16)
    parts = lax.all_to_all(term, ("x", "z"), 0, 0, tiled=True)

    activations, grad, piece = pl.pallas_call(
        middle,
        in_specs=[vmem()] * 3,
        out_specs=[vmem()] * 3,
        out_shape=[
            jax.ShapeDtypeStruct((TILE, WIDTH), BF16),
            jax.ShapeDtypeStruct((X * Z, TILE, CHUNK), BF16),
            jax.ShapeDtypeStruct((WIDTH, WIDTH), BF16),
        ],
        compiler_params=params(),
        name="middle",
    )(parts, weight, cotangent)

    grad_mine = lax.all_to_all(grad, ("x", "z"), 0, 0, tiled=True)
    piece = scatter(piece, "x")
    piece = double4(piece, "y")
    grad_mine, piece = lax.optimization_barrier((grad_mine, piece))

    grad_other = exchange(grad_mine, "core", 1)
    piece = double(piece, "y", Y - 1)
    back = pl.pallas_call(
        backward_tiles,
        in_specs=[smem(), smem()] + [vmem()] * (2 + X),
        out_specs=vmem(),
        out_shape=jax.ShapeDtypeStruct((COL_TILES, TILE, CHUNK), BF16),
        scratch_shapes=[pltpu.VMEM((COL_TILES, TILE, CHUNK), F32)],
        compiler_params=params(),
        name="backward_tiles",
    )(place, index, grad_mine, grad_other, *tiles)
    back, piece = lax.optimization_barrier((back, piece))
    back = lax.all_to_all(back, ("y", "x"), 0, 0, tiled=True)
    for distance in (1, 2, Z - 1):
        piece = double(piece, "z", distance)
    piece = double(piece, "core", 1)
    back, piece = lax.optimization_barrier((back, piece))

    input_grad = pl.pallas_call(
        last,
        in_specs=[vmem()] * 2,
        out_specs=vmem(),
        out_shape=jax.ShapeDtypeStruct((TILE, WIDTH), BF16),
        compiler_params=params(),
        name="last",
    )(back, weight)

    whole = lax.all_to_all(jnp.broadcast_to(piece[None], (X, *piece.shape)), "x", 0, 0, tiled=True)
    nodes = TILE * Y * X * Z * CORES
    weight_grad = whole.reshape(WIDTH, WIDTH).astype(F32) * (1.0 / math.sqrt(nodes))
    return (activations, input_grad, weight_grad)


def solution(mesh):
    axes = Mesh(mesh.devices.reshape(Y, X, Z, CORES), ("y", "x", "z", "core"))
    row, col = ("y", "x"), ("z", "core")
    placed = (
        P(col + row, None),
        P(),
        P(row + col, None),
        P(row, col, None, None, None),
        P(row, col, None),
        P(row, col, None),
        P(row, col, None),
    )
    return jax.shard_map(
        body,
        mesh=axes,
        in_specs=placed,
        out_specs=(P(row + col, None), P(col + row, None), P()),
        check_vma=False,
    )
```

```python
import math

import jax
import jax.numpy as jnp
from jax import lax
from jax.experimental import pallas as pl
from jax.experimental.pallas import tpu as pltpu
from jax.sharding import Mesh, PartitionSpec as P

Y_HIGH, Y_LOW, X, Z, CORES = 4, 2, 4, 8, 2
Y = Y_HIGH * Y_LOW
ROW = ("y_high", "y_low", "x")
COL = ("z", "core")
TILE = 128
SLOTS = 8
WIDTH = 512
CHUNK = WIDTH // X
ROW_TILES = Z * CORES
COL_TILES = Y * X
INDEX_ROWS = 16
BF16 = jnp.bfloat16
F32 = jnp.float32


def params():
    return pltpu.CompilerParams(vmem_limit_bytes=24 * 1024 * 1024)


def vmem():
    return pl.BlockSpec(memory_space=pltpu.VMEM)


def smem():
    return pl.BlockSpec(memory_space=pltpu.SMEM)


def spread(features_ref, out_ref):
    for chunk in range(X):
        piece = features_ref[:, chunk * CHUNK : (chunk + 1) * CHUNK]
        for y in range(Y):
            out_ref[y * X + chunk] = piece


def forward_tiles(place_ref, index_ref, panel_ref, *refs):
    tiles_refs, (mine_ref, other_ref, total) = refs[:X], refs[X:]
    core = place_ref[0]
    for step in range(X):
        block = place_ref[1] ^ step
        total[...] = jnp.zeros_like(total)
        for slot in range(SLOTS):
            row = index_ref[step, slot]
            col = index_ref[step, SLOTS + slot]
            valid = index_ref[step, 2 * SLOTS + slot]
            tile = tiles_refs[step][slot * TILE : (slot + 1) * TILE, :]
            product = jnp.dot(tile, panel_ref[col], preferred_element_type=F32)
            total[row] += jnp.where(valid > 0, product, 0.0)
        for pair in range(Z):
            mine_ref[block * Z + pair] = total[2 * pair + core].astype(BF16)
            other_ref[block * Z + pair] = total[2 * pair + 1 - core].astype(BF16)


def middle(core_ref, parts_ref, weight_ref, cotangent_ref, act_ref, grad_ref, keep_ref, send_ref):
    chunks = []
    for chunk in range(X):
        total = parts_ref[chunk * Z].astype(F32)
        for z in range(1, Z):
            total += parts_ref[chunk * Z + z].astype(F32)
        chunks.append(total)
    summed = jnp.concatenate(chunks, axis=1)
    high = summed.astype(BF16)
    low = (summed - high.astype(F32)).astype(BF16)
    weight = weight_ref[...]
    aggregated = jnp.dot(high, weight, preferred_element_type=F32) + jnp.dot(
        low, weight, preferred_element_type=F32
    )
    sig = jax.nn.sigmoid(aggregated)
    act_ref[...] = (aggregated * sig).astype(BF16)
    grad = (cotangent_ref[...].astype(F32) * sig * (1.0 + aggregated * (1.0 - sig))).astype(BF16)
    for chunk in range(X):
        piece = grad[:, chunk * CHUNK : (chunk + 1) * CHUNK]
        for z in range(Z):
            grad_ref[chunk * Z + z] = piece
    weight_part = lax.dot_general(
        high, grad, (((0,), (0,)), ((), ())), preferred_element_type=F32
    ).astype(BF16)
    low_half, high_half = weight_part[: WIDTH // 2], weight_part[WIDTH // 2 :]
    upper = core_ref[0] == 1
    keep_ref[...] = jnp.where(upper, high_half, low_half)
    send_ref[...] = jnp.where(upper, low_half, high_half)


def backward_tiles(place_ref, index_ref, mine_ref, other_ref, *refs):
    tiles_refs, (out_ref, total) = refs[:X], refs[X:]
    core = place_ref[0]
    total[...] = jnp.zeros_like(total)
    for step in range(X):
        block = place_ref[1] ^ step
        for slot in range(SLOTS):
            row = index_ref[step, slot]
            col = index_ref[step, SLOTS + slot]
            valid = index_ref[step, 2 * SLOTS + slot]
            at = block * Z + row // 2
            panel = jnp.where(row % 2 == core, mine_ref[at], other_ref[at])
            tile = tiles_refs[step][slot * TILE : (slot + 1) * TILE, :]
            product = lax.dot_general(
                tile, panel, (((0,), (0,)), ((), ())), preferred_element_type=F32
            )
            total[col] += jnp.where(valid > 0, product, 0.0)
    for tile in range(COL_TILES):
        out_ref[tile] = total[tile].astype(BF16)


def last(parts_ref, weight_ref, out_ref):
    chunks = []
    for chunk in range(X):
        total = parts_ref[chunk].astype(F32)
        for y in range(1, Y):
            total += parts_ref[y * X + chunk].astype(F32)
        chunks.append(total)
    summed = jnp.concatenate(chunks, axis=1).astype(BF16)
    out_ref[...] = lax.dot_general(
        summed, weight_ref[...], (((1,), (1,)), ((), ())), preferred_element_type=F32
    ).astype(BF16)


def place_rows(place_ref, mine_ref, other_ref, out_ref):
    core = place_ref[0]
    half, share = WIDTH // CORES, WIDTH // (Y_HIGH * CORES)
    scale = 1.0 / math.sqrt(TILE * Y * X * Z * CORES)
    for y in range(Y_HIGH):
        for side, ref in ((core, mine_ref), (1 - core, other_ref)):
            start = pl.multiple_of(side * half + y * share, share)
            out_ref[pl.ds(start, share), :] = ref[y].astype(F32) * scale


def exchange(array, axis, distance):
    size = lax.axis_size(axis)
    return lax.ppermute(array, axis, [(i, i ^ distance) for i in range(size)])


def scatter(array, axis):
    size, place = lax.axis_size(axis), lax.axis_index(axis)
    shares = array.reshape(size, array.shape[0] // size, array.shape[1])

    def share(distance):
        return lax.dynamic_index_in_dim(shares, place ^ distance, 0, keepdims=False)

    total = share(0).astype(F32)
    for distance in range(1, size):
        total = total + exchange(share(distance), axis, distance).astype(F32)
    return total.astype(BF16)


def double(array, axis, distance):
    return (array.astype(F32) + exchange(array, axis, distance).astype(F32)).astype(BF16)


def double4(array, axis):
    one, two, three = (exchange(array, axis, distance).astype(F32) for distance in (1, 2, 3))
    return ((array.astype(F32) + one) + (two + three)).astype(BF16)


def body(features, weight, cotangent, tile_values, tile_rows, tile_cols, tile_valid):
    place = jnp.stack([lax.axis_index("core"), lax.axis_index("x")]).astype(jnp.int32)

    chunks = pl.pallas_call(
        spread,
        in_specs=[vmem()],
        out_specs=vmem(),
        out_shape=jax.ShapeDtypeStruct((COL_TILES, TILE, CHUNK), BF16),
        compiler_params=params(),
        name="spread",
    )(features)
    panel = lax.all_to_all(chunks, ROW, 0, 0, tiled=True)

    index = jnp.concatenate(
        [tile_rows.reshape(-1), tile_cols.reshape(-1), tile_valid.reshape(-1)]
    ).astype(BF16)
    index = jnp.pad(index[None, :], ((0, INDEX_ROWS - 1), (0, TILE - 3 * SLOTS)))
    tiles = jnp.concatenate([tile_values.reshape(SLOTS * TILE, TILE), index], axis=0)
    tiles = [tiles] + [exchange(tiles, "x", distance) for distance in range(1, X)]
    index = jnp.stack([t[SLOTS * TILE, : 3 * SLOTS] for t in tiles]).astype(jnp.int32)
    limit = jnp.repeat(jnp.array([ROW_TILES - 1, COL_TILES - 1, 1], jnp.int32), SLOTS)
    index = jnp.clip(index, 0, limit[None, :])

    mine, other = pl.pallas_call(
        forward_tiles,
        in_specs=[smem(), smem()] + [vmem()] * (1 + X),
        out_specs=[vmem()] * 2,
        out_shape=[jax.ShapeDtypeStruct((X * Z, TILE, CHUNK), BF16)] * 2,
        scratch_shapes=[pltpu.VMEM((ROW_TILES, TILE, CHUNK), F32)],
        compiler_params=params(),
        name="forward_tiles",
    )(place, index, panel, *tiles)
    term = (mine.astype(F32) + exchange(other, "core", 1).astype(F32)).astype(BF16)
    parts = lax.all_to_all(term, ("x", "z"), 0, 0, tiled=True)

    half = WIDTH // CORES
    activations, grad, weight_keep, weight_send = pl.pallas_call(
        middle,
        in_specs=[smem()] + [vmem()] * 3,
        out_specs=[vmem()] * 4,
        out_shape=[
            jax.ShapeDtypeStruct((TILE, WIDTH), BF16),
            jax.ShapeDtypeStruct((X * Z, TILE, CHUNK), BF16),
            jax.ShapeDtypeStruct((half, WIDTH), BF16),
            jax.ShapeDtypeStruct((half, WIDTH), BF16),
        ],
        compiler_params=params(),
        name="middle",
    )(place, parts, weight, cotangent)

    grad_mine = lax.all_to_all(grad, ("x", "z"), 0, 0, tiled=True)
    piece = weight_keep.astype(F32) + exchange(weight_send, "core", 1).astype(F32)
    piece = piece.astype(BF16)
    piece = scatter(piece, "y_high")
    piece = double(piece, "y_low", 1)
    piece = double(piece, "x", 1)
    grad_mine, piece = lax.optimization_barrier((grad_mine, piece))

    grad_other = exchange(grad_mine, "core", 1)
    back = pl.pallas_call(
        backward_tiles,
        in_specs=[smem(), smem()] + [vmem()] * (2 + X),
        out_specs=vmem(),
        out_shape=jax.ShapeDtypeStruct((COL_TILES, TILE, CHUNK), BF16),
        scratch_shapes=[pltpu.VMEM((COL_TILES, TILE, CHUNK), F32)],
        compiler_params=params(),
        name="backward_tiles",
    )(place, index, grad_mine, grad_other, *tiles)
    back, piece = lax.optimization_barrier((back, piece))
    back = lax.all_to_all(back, ROW, 0, 0, tiled=True)
    piece = double4(piece, "z")
    piece = double(piece, "z", Z - 1)
    piece = double(piece, "x", X - 1)
    back, piece = lax.optimization_barrier((back, piece))

    input_grad = pl.pallas_call(
        last,
        in_specs=[vmem()] * 2,
        out_specs=vmem(),
        out_shape=jax.ShapeDtypeStruct((TILE, WIDTH), BF16),
        compiler_params=params(),
        name="last",
    )(back, weight)

    share = WIDTH // (Y_HIGH * CORES)
    piece = jnp.broadcast_to(piece[None], (Y_HIGH, share, WIDTH))
    whole = lax.all_to_all(piece, "y_high", 0, 0, tiled=True)
    weight_grad = pl.pallas_call(
        place_rows,
        in_specs=[smem()] + [vmem()] * 2,
        out_specs=vmem(),
        out_shape=jax.ShapeDtypeStruct((WIDTH, WIDTH), F32),
        compiler_params=params(),
        name="place_rows",
    )(place, whole, exchange(whole, "core", 1))
    return (activations, input_grad, weight_grad)


def solution(mesh):
    axes = Mesh(mesh.devices.reshape(Y_HIGH, Y_LOW, X, Z, CORES), ROW + COL)
    placed = (
        P(COL + ROW, None),
        P(),
        P(ROW + COL, None),
        P(ROW, COL, None, None, None),
        P(ROW, COL, None),
        P(ROW, COL, None),
        P(ROW, COL, None),
    )
    return jax.shard_map(
        body,
        mesh=axes,
        in_specs=placed,
        out_specs=(P(ROW + COL, None), P(COL + ROW, None), P()),
        check_vma=False,
    )
```

```python
import math

import jax
import jax.numpy as jnp
from jax import lax
from jax.experimental import pallas as pl
from jax.experimental.pallas import tpu as pltpu
from jax.sharding import Mesh, PartitionSpec as P

Y_HIGH, Y_LOW, X, Z, CORES = 2, 4, 4, 8, 2
Y = Y_HIGH * Y_LOW
ROW = ("y_high", "y_low", "x")
COL = ("z", "core")
TILE = 128
SLOTS = 8
WIDTH = 512
CHUNK = WIDTH // X
ROW_TILES = Z * CORES
COL_TILES = Y * X
INDEX_ROWS = 16
BF16 = jnp.bfloat16
F32 = jnp.float32


def params():
    return pltpu.CompilerParams(vmem_limit_bytes=24 * 1024 * 1024)


def vmem():
    return pl.BlockSpec(memory_space=pltpu.VMEM)


def smem():
    return pl.BlockSpec(memory_space=pltpu.SMEM)


def spread(features_ref, out_ref):
    for chunk in range(X):
        piece = features_ref[:, chunk * CHUNK : (chunk + 1) * CHUNK]
        for y in range(Y):
            out_ref[y * X + chunk] = piece


def forward_tiles(place_ref, index_ref, panel_ref, *refs):
    tiles_refs, (mine_ref, other_ref, total) = refs[:X], refs[X:]
    core = place_ref[0]
    for step in range(X):
        block = place_ref[1] ^ step
        total[...] = jnp.zeros_like(total)
        for slot in range(SLOTS):
            row = index_ref[step, slot]
            col = index_ref[step, SLOTS + slot]
            valid = index_ref[step, 2 * SLOTS + slot]
            tile = tiles_refs[step][slot * TILE : (slot + 1) * TILE, :]
            product = jnp.dot(tile, panel_ref[col], preferred_element_type=F32)
            total[row] += jnp.where(valid > 0, product, 0.0)
        for pair in range(Z):
            mine_ref[block * Z + pair] = total[2 * pair + core].astype(BF16)
            other_ref[block * Z + pair] = total[2 * pair + 1 - core].astype(BF16)


def middle(core_ref, parts_ref, weight_ref, cotangent_ref, act_ref, grad_ref, keep_ref, send_ref):
    chunks = []
    for chunk in range(X):
        total = parts_ref[chunk * Z].astype(F32)
        for z in range(1, Z):
            total += parts_ref[chunk * Z + z].astype(F32)
        chunks.append(total)
    summed = jnp.concatenate(chunks, axis=1)
    high = summed.astype(BF16)
    low = (summed - high.astype(F32)).astype(BF16)
    weight = weight_ref[...]
    aggregated = jnp.dot(high, weight, preferred_element_type=F32) + jnp.dot(
        low, weight, preferred_element_type=F32
    )
    sig = jax.nn.sigmoid(aggregated)
    act_ref[...] = (aggregated * sig).astype(BF16)
    grad = (cotangent_ref[...].astype(F32) * sig * (1.0 + aggregated * (1.0 - sig))).astype(BF16)
    for chunk in range(X):
        piece = grad[:, chunk * CHUNK : (chunk + 1) * CHUNK]
        for z in range(Z):
            grad_ref[chunk * Z + z] = piece
    weight_part = lax.dot_general(
        high, grad, (((0,), (0,)), ((), ())), preferred_element_type=F32
    ).astype(BF16)
    low_half, high_half = weight_part[: WIDTH // 2], weight_part[WIDTH // 2 :]
    upper = core_ref[0] == 1
    keep_ref[...] = jnp.where(upper, high_half, low_half)
    send_ref[...] = jnp.where(upper, low_half, high_half)


def backward_tiles(place_ref, index_ref, mine_ref, other_ref, *refs):
    tiles_refs, (out_ref, total) = refs[:X], refs[X:]
    core = place_ref[0]
    total[...] = jnp.zeros_like(total)
    for step in range(X):
        block = place_ref[1] ^ step
        for slot in range(SLOTS):
            row = index_ref[step, slot]
            col = index_ref[step, SLOTS + slot]
            valid = index_ref[step, 2 * SLOTS + slot]
            at = block * Z + row // 2
            panel = jnp.where(row % 2 == core, mine_ref[at], other_ref[at])
            tile = tiles_refs[step][slot * TILE : (slot + 1) * TILE, :]
            product = lax.dot_general(
                tile, panel, (((0,), (0,)), ((), ())), preferred_element_type=F32
            )
            total[col] += jnp.where(valid > 0, product, 0.0)
    for tile in range(COL_TILES):
        out_ref[tile] = total[tile].astype(BF16)


def last(parts_ref, weight_ref, out_ref):
    chunks = []
    for chunk in range(X):
        total = parts_ref[chunk].astype(F32)
        for y in range(1, Y):
            total += parts_ref[y * X + chunk].astype(F32)
        chunks.append(total)
    summed = jnp.concatenate(chunks, axis=1).astype(BF16)
    out_ref[...] = lax.dot_general(
        summed, weight_ref[...], (((1,), (1,)), ((), ())), preferred_element_type=F32
    ).astype(BF16)


def place_rows(place_ref, mine_ref, other_ref, out_ref):
    core = place_ref[0]
    half, share = WIDTH // CORES, WIDTH // (Y_LOW * CORES)
    scale = 1.0 / math.sqrt(TILE * Y * X * Z * CORES)
    for y in range(Y_LOW):
        for side, ref in ((core, mine_ref), (1 - core, other_ref)):
            start = pl.multiple_of(side * half + y * share, share)
            out_ref[pl.ds(start, share), :] = ref[y].astype(F32) * scale


def exchange(array, axis, distance):
    size = lax.axis_size(axis)
    return lax.ppermute(array, axis, [(i, i ^ distance) for i in range(size)])


def scatter(array, axis):
    size, place = lax.axis_size(axis), lax.axis_index(axis)
    shares = array.reshape(size, array.shape[0] // size, array.shape[1])

    def share(distance):
        return lax.dynamic_index_in_dim(shares, place ^ distance, 0, keepdims=False)

    total = share(0).astype(F32)
    for distance in range(1, size):
        total = total + exchange(share(distance), axis, distance).astype(F32)
    return total.astype(BF16)


def double(array, axis, distance):
    return (array.astype(F32) + exchange(array, axis, distance).astype(F32)).astype(BF16)


def double4(array, axis):
    one, two, three = (exchange(array, axis, distance).astype(F32) for distance in (1, 2, 3))
    return ((array.astype(F32) + one) + (two + three)).astype(BF16)


def body(features, weight, cotangent, tile_values, tile_rows, tile_cols, tile_valid):
    place = jnp.stack([lax.axis_index("core"), lax.axis_index("x")]).astype(jnp.int32)

    chunks = pl.pallas_call(
        spread,
        in_specs=[vmem()],
        out_specs=vmem(),
        out_shape=jax.ShapeDtypeStruct((COL_TILES, TILE, CHUNK), BF16),
        compiler_params=params(),
        name="spread",
    )(features)
    panel = lax.all_to_all(chunks, ROW, 0, 0, tiled=True)

    index = jnp.concatenate(
        [tile_rows.reshape(-1), tile_cols.reshape(-1), tile_valid.reshape(-1)]
    ).astype(BF16)
    index = jnp.pad(index[None, :], ((0, INDEX_ROWS - 1), (0, TILE - 3 * SLOTS)))
    tiles = jnp.concatenate([tile_values.reshape(SLOTS * TILE, TILE), index], axis=0)
    tiles = [tiles] + [exchange(tiles, "x", distance) for distance in range(1, X)]
    index = jnp.stack([t[SLOTS * TILE, : 3 * SLOTS] for t in tiles]).astype(jnp.int32)
    limit = jnp.repeat(jnp.array([ROW_TILES - 1, COL_TILES - 1, 1], jnp.int32), SLOTS)
    index = jnp.clip(index, 0, limit[None, :])

    mine, other = pl.pallas_call(
        forward_tiles,
        in_specs=[smem(), smem()] + [vmem()] * (1 + X),
        out_specs=[vmem()] * 2,
        out_shape=[jax.ShapeDtypeStruct((X * Z, TILE, CHUNK), BF16)] * 2,
        scratch_shapes=[pltpu.VMEM((ROW_TILES, TILE, CHUNK), F32)],
        compiler_params=params(),
        name="forward_tiles",
    )(place, index, panel, *tiles)
    term = (mine.astype(F32) + exchange(other, "core", 1).astype(F32)).astype(BF16)
    parts = lax.all_to_all(term, ("x", "z"), 0, 0, tiled=True)

    half = WIDTH // CORES
    activations, grad, weight_keep, weight_send = pl.pallas_call(
        middle,
        in_specs=[smem()] + [vmem()] * 3,
        out_specs=[vmem()] * 4,
        out_shape=[
            jax.ShapeDtypeStruct((TILE, WIDTH), BF16),
            jax.ShapeDtypeStruct((X * Z, TILE, CHUNK), BF16),
            jax.ShapeDtypeStruct((half, WIDTH), BF16),
            jax.ShapeDtypeStruct((half, WIDTH), BF16),
        ],
        compiler_params=params(),
        name="middle",
    )(place, parts, weight, cotangent)

    grad_mine = lax.all_to_all(grad, ("x", "z"), 0, 0, tiled=True)
    piece = weight_keep.astype(F32) + exchange(weight_send, "core", 1).astype(F32)
    piece = piece.astype(BF16)
    piece = scatter(piece, "y_low")
    piece = double(piece, "y_high", 1)
    piece = double(piece, "x", 1)
    grad_mine, piece = lax.optimization_barrier((grad_mine, piece))

    grad_other = exchange(grad_mine, "core", 1)
    back = pl.pallas_call(
        backward_tiles,
        in_specs=[smem(), smem()] + [vmem()] * (2 + X),
        out_specs=vmem(),
        out_shape=jax.ShapeDtypeStruct((COL_TILES, TILE, CHUNK), BF16),
        scratch_shapes=[pltpu.VMEM((COL_TILES, TILE, CHUNK), F32)],
        compiler_params=params(),
        name="backward_tiles",
    )(place, index, grad_mine, grad_other, *tiles)
    back, piece = lax.optimization_barrier((back, piece))
    back = lax.all_to_all(back, ROW, 0, 0, tiled=True)
    piece = double4(piece, "z")
    piece = double(piece, "z", Z - 1)
    piece = double(piece, "x", X - 1)
    back, piece = lax.optimization_barrier((back, piece))

    input_grad = pl.pallas_call(
        last,
        in_specs=[vmem()] * 2,
        out_specs=vmem(),
        out_shape=jax.ShapeDtypeStruct((TILE, WIDTH), BF16),
        compiler_params=params(),
        name="last",
    )(back, weight)

    share = WIDTH // (Y_LOW * CORES)
    piece = jnp.broadcast_to(piece[None], (Y_LOW, share, WIDTH))
    whole = lax.all_to_all(piece, "y_low", 0, 0, tiled=True)
    weight_grad = pl.pallas_call(
        place_rows,
        in_specs=[smem()] + [vmem()] * 2,
        out_specs=vmem(),
        out_shape=jax.ShapeDtypeStruct((WIDTH, WIDTH), F32),
        compiler_params=params(),
        name="place_rows",
    )(place, whole, exchange(whole, "core", 1))
    return (activations, input_grad, weight_grad)


def solution(mesh):
    axes = Mesh(mesh.devices.reshape(Y_HIGH, Y_LOW, X, Z, CORES), ROW + COL)
    placed = (
        P(COL + ROW, None),
        P(),
        P(ROW + COL, None),
        P(ROW, COL, None, None, None),
        P(ROW, COL, None),
        P(ROW, COL, None),
        P(ROW, COL, None),
    )
    return jax.shard_map(
        body,
        mesh=axes,
        in_specs=placed,
        out_specs=(P(ROW + COL, None), P(COL + ROW, None), P()),
        check_vma=False,
    )
```

```python
import math

import jax
import jax.numpy as jnp
from jax import lax
from jax.experimental import pallas as pl
from jax.experimental.pallas import tpu as pltpu
from jax.sharding import Mesh, PartitionSpec as P

Y_HIGH, Y_LOW, X, Z, CORES = 2, 4, 4, 8, 2
Y = Y_HIGH * Y_LOW
ROW = ("y_high", "y_low", "x")
COL = ("z", "core")
TILE = 128
SLOTS = 8
WIDTH = 512
CHUNK = WIDTH // X
ROW_TILES = Z * CORES
COL_TILES = Y * X
INDEX_ROWS = 16
BF16 = jnp.bfloat16
F32 = jnp.float32


def params():
    return pltpu.CompilerParams(vmem_limit_bytes=24 * 1024 * 1024)


def vmem():
    return pl.BlockSpec(memory_space=pltpu.VMEM)


def smem():
    return pl.BlockSpec(memory_space=pltpu.SMEM)


def spread(features_ref, out_ref):
    for chunk in range(X):
        piece = features_ref[:, chunk * CHUNK : (chunk + 1) * CHUNK]
        for y in range(Y):
            out_ref[y * X + chunk] = piece


def forward_tiles(place_ref, index_ref, panel_ref, *refs):
    tiles_refs, (mine_ref, other_ref, total) = refs[:X], refs[X:]
    core = place_ref[0]
    for step in range(X):
        block = place_ref[1] ^ step
        total[...] = jnp.zeros_like(total)
        for slot in range(SLOTS):
            row = index_ref[step, slot]
            col = index_ref[step, SLOTS + slot]
            valid = index_ref[step, 2 * SLOTS + slot]
            tile = tiles_refs[step][slot * TILE : (slot + 1) * TILE, :]
            product = jnp.dot(tile, panel_ref[col], preferred_element_type=F32)
            total[row] += jnp.where(valid > 0, product, 0.0)
        for pair in range(Z):
            mine_ref[block * Z + pair] = total[2 * pair + core].astype(BF16)
            other_ref[block * Z + pair] = total[2 * pair + 1 - core].astype(BF16)


def middle(core_ref, parts_ref, weight_ref, cotangent_ref, act_ref, grad_ref, keep_ref, send_ref):
    chunks = []
    for chunk in range(X):
        total = parts_ref[chunk * Z].astype(F32)
        for z in range(1, Z):
            total += parts_ref[chunk * Z + z].astype(F32)
        chunks.append(total)
    summed = jnp.concatenate(chunks, axis=1)
    high = summed.astype(BF16)
    low = (summed - high.astype(F32)).astype(BF16)
    weight = weight_ref[...]
    aggregated = jnp.dot(high, weight, preferred_element_type=F32) + jnp.dot(
        low, weight, preferred_element_type=F32
    )
    sig = jax.nn.sigmoid(aggregated)
    act_ref[...] = (aggregated * sig).astype(BF16)
    grad = (cotangent_ref[...].astype(F32) * sig * (1.0 + aggregated * (1.0 - sig))).astype(BF16)
    for chunk in range(X):
        piece = grad[:, chunk * CHUNK : (chunk + 1) * CHUNK]
        for z in range(Z):
            grad_ref[chunk * Z + z] = piece
    weight_part = lax.dot_general(
        high, grad, (((0,), (0,)), ((), ())), preferred_element_type=F32
    ).astype(BF16)
    low_half, high_half = weight_part[: WIDTH // 2], weight_part[WIDTH // 2 :]
    upper = core_ref[0] == 1
    keep_ref[...] = jnp.where(upper, high_half, low_half)
    send_ref[...] = jnp.where(upper, low_half, high_half)


def backward_tiles(place_ref, index_ref, mine_ref, other_ref, *refs):
    tiles_refs, (out_ref, total) = refs[:X], refs[X:]
    core = place_ref[0]
    total[...] = jnp.zeros_like(total)
    for step in range(X):
        block = place_ref[1] ^ step
        for slot in range(SLOTS):
            row = index_ref[step, slot]
            col = index_ref[step, SLOTS + slot]
            valid = index_ref[step, 2 * SLOTS + slot]
            at = block * Z + row // 2
            panel = jnp.where(row % 2 == core, mine_ref[at], other_ref[at])
            tile = tiles_refs[step][slot * TILE : (slot + 1) * TILE, :]
            product = lax.dot_general(
                tile, panel, (((0,), (0,)), ((), ())), preferred_element_type=F32
            )
            total[col] += jnp.where(valid > 0, product, 0.0)
    for tile in range(COL_TILES):
        out_ref[tile] = total[tile].astype(BF16)


def last(parts_ref, weight_ref, out_ref):
    chunks = []
    for chunk in range(X):
        total = parts_ref[chunk].astype(F32)
        for y in range(1, Y):
            total += parts_ref[y * X + chunk].astype(F32)
        chunks.append(total)
    summed = jnp.concatenate(chunks, axis=1).astype(BF16)
    out_ref[...] = lax.dot_general(
        summed, weight_ref[...], (((1,), (1,)), ((), ())), preferred_element_type=F32
    ).astype(BF16)


def place_rows(place_ref, mine_ref, other_ref, out_ref):
    core = place_ref[0]
    half, share = WIDTH // CORES, WIDTH // (Y_LOW * CORES)
    scale = 1.0 / math.sqrt(TILE * Y * X * Z * CORES)
    for y in range(Y_LOW):
        for side, ref in ((core, mine_ref), (1 - core, other_ref)):
            start = pl.multiple_of(side * half + (y ^ place_ref[2]) * share, share)
            out_ref[pl.ds(start, share), :] = ref[y].astype(F32) * scale


def exchange(array, axis, distance):
    size = lax.axis_size(axis)
    return lax.ppermute(array, axis, [(i, i ^ distance) for i in range(size)])


def scatter(array, axis, flip):
    size, place = lax.axis_size(axis), lax.axis_index(axis) ^ flip
    shares = array.reshape(size, array.shape[0] // size, array.shape[1])

    def share(distance):
        return lax.dynamic_index_in_dim(shares, place ^ distance, 0, keepdims=False)

    total = share(0).astype(F32)
    for distance in range(1, size):
        total = total + exchange(share(distance), axis, distance).astype(F32)
    return total.astype(BF16)


def double(array, axis, distance):
    return (array.astype(F32) + exchange(array, axis, distance).astype(F32)).astype(BF16)


def double4(array, axis):
    one, two, three = (exchange(array, axis, distance).astype(F32) for distance in (1, 2, 3))
    return ((array.astype(F32) + one) + (two + three)).astype(BF16)


def body(features, weight, cotangent, tile_values, tile_rows, tile_cols, tile_valid):
    flip = lax.axis_index("y_high") * (Y_LOW - 1)
    place = jnp.stack([lax.axis_index("core"), lax.axis_index("x"), flip]).astype(jnp.int32)

    chunks = pl.pallas_call(
        spread,
        in_specs=[vmem()],
        out_specs=vmem(),
        out_shape=jax.ShapeDtypeStruct((COL_TILES, TILE, CHUNK), BF16),
        compiler_params=params(),
        name="spread",
    )(features)
    panel = lax.all_to_all(chunks, ROW, 0, 0, tiled=True)

    index = jnp.concatenate(
        [tile_rows.reshape(-1), tile_cols.reshape(-1), tile_valid.reshape(-1)]
    ).astype(BF16)
    index = jnp.pad(index[None, :], ((0, INDEX_ROWS - 1), (0, TILE - 3 * SLOTS)))
    tiles = jnp.concatenate([tile_values.reshape(SLOTS * TILE, TILE), index], axis=0)
    tiles = [tiles] + [exchange(tiles, "x", distance) for distance in range(1, X)]
    index = jnp.stack([t[SLOTS * TILE, : 3 * SLOTS] for t in tiles]).astype(jnp.int32)
    limit = jnp.repeat(jnp.array([ROW_TILES - 1, COL_TILES - 1, 1], jnp.int32), SLOTS)
    index = jnp.clip(index, 0, limit[None, :])

    mine, other = pl.pallas_call(
        forward_tiles,
        in_specs=[smem(), smem()] + [vmem()] * (1 + X),
        out_specs=[vmem()] * 2,
        out_shape=[jax.ShapeDtypeStruct((X * Z, TILE, CHUNK), BF16)] * 2,
        scratch_shapes=[pltpu.VMEM((ROW_TILES, TILE, CHUNK), F32)],
        compiler_params=params(),
        name="forward_tiles",
    )(place, index, panel, *tiles)
    term = (mine.astype(F32) + exchange(other, "core", 1).astype(F32)).astype(BF16)
    parts = lax.all_to_all(term, ("x", "z"), 0, 0, tiled=True)

    half = WIDTH // CORES
    activations, grad, weight_keep, weight_send = pl.pallas_call(
        middle,
        in_specs=[smem()] + [vmem()] * 3,
        out_specs=[vmem()] * 4,
        out_shape=[
            jax.ShapeDtypeStruct((TILE, WIDTH), BF16),
            jax.ShapeDtypeStruct((X * Z, TILE, CHUNK), BF16),
            jax.ShapeDtypeStruct((half, WIDTH), BF16),
            jax.ShapeDtypeStruct((half, WIDTH), BF16),
        ],
        compiler_params=params(),
        name="middle",
    )(place, parts, weight, cotangent)

    grad_mine = lax.all_to_all(grad, ("x", "z"), 0, 0, tiled=True)
    piece = weight_keep.astype(F32) + exchange(weight_send, "core", 1).astype(F32)
    piece = piece.astype(BF16)
    piece = scatter(piece, "y_low", flip)
    piece = double(piece, ("y_high", "y_low"), Y - 1)
    piece = double(piece, "x", 1)
    grad_mine, piece = lax.optimization_barrier((grad_mine, piece))

    grad_other = exchange(grad_mine, "core", 1)
    back = pl.pallas_call(
        backward_tiles,
        in_specs=[smem(), smem()] + [vmem()] * (2 + X),
        out_specs=vmem(),
        out_shape=jax.ShapeDtypeStruct((COL_TILES, TILE, CHUNK), BF16),
        scratch_shapes=[pltpu.VMEM((COL_TILES, TILE, CHUNK), F32)],
        compiler_params=params(),
        name="backward_tiles",
    )(place, index, grad_mine, grad_other, *tiles)
    back, piece = lax.optimization_barrier((back, piece))
    back = lax.all_to_all(back, ROW, 0, 0, tiled=True)
    piece = double4(piece, "z")
    piece = double(piece, "z", Z - 1)
    piece = double(piece, "x", X - 1)
    back, piece = lax.optimization_barrier((back, piece))

    input_grad = pl.pallas_call(
        last,
        in_specs=[vmem()] * 2,
        out_specs=vmem(),
        out_shape=jax.ShapeDtypeStruct((TILE, WIDTH), BF16),
        compiler_params=params(),
        name="last",
    )(back, weight)

    share = WIDTH // (Y_LOW * CORES)
    piece = jnp.broadcast_to(piece[None], (Y_LOW, share, WIDTH))
    whole = lax.all_to_all(piece, "y_low", 0, 0, tiled=True)
    weight_grad = pl.pallas_call(
        place_rows,
        in_specs=[smem()] + [vmem()] * 2,
        out_specs=vmem(),
        out_shape=jax.ShapeDtypeStruct((WIDTH, WIDTH), F32),
        compiler_params=params(),
        name="place_rows",
    )(place, whole, exchange(whole, "core", 1))
    return (activations, input_grad, weight_grad)


def solution(mesh):
    axes = Mesh(mesh.devices.reshape(Y_HIGH, Y_LOW, X, Z, CORES), ROW + COL)
    placed = (
        P(COL + ROW, None),
        P(),
        P(ROW + COL, None),
        P(ROW, COL, None, None, None),
        P(ROW, COL, None),
        P(ROW, COL, None),
        P(ROW, COL, None),
    )
    return jax.shard_map(
        body,
        mesh=axes,
        in_specs=placed,
        out_specs=(P(ROW + COL, None), P(COL + ROW, None), P()),
        check_vma=False,
    )
```

```python
import functools
import math

import jax
import jax.numpy as jnp
from jax import lax
from jax.experimental import pallas as pl
from jax.experimental.pallas import tpu as pltpu
from jax.sharding import Mesh, PartitionSpec as P

Y_HIGH, Y_LOW, X, Z, CORES = 2, 4, 4, 8, 2
Y = Y_HIGH * Y_LOW
ROW = ("y_high", "y_low", "x")
COL = ("z", "core")
TILE = 128
SLOTS = 8
WIDTH = 512
CHUNK = WIDTH // X
ROW_TILES = Z * CORES
COL_TILES = Y * X
INDEX_ROWS = 16
BF16 = jnp.bfloat16
F32 = jnp.float32


def params():
    return pltpu.CompilerParams(vmem_limit_bytes=24 * 1024 * 1024)


def vmem():
    return pl.BlockSpec(memory_space=pltpu.VMEM)


def smem():
    return pl.BlockSpec(memory_space=pltpu.SMEM)


def spread(places, in_ref, out_ref):
    for place, chunk in enumerate(places):
        out_ref[place] = in_ref[:, chunk * CHUNK : (chunk + 1) * CHUNK]


def spread_chunks(array, places, name):
    return pl.pallas_call(
        functools.partial(spread, places),
        in_specs=[vmem()],
        out_specs=vmem(),
        out_shape=jax.ShapeDtypeStruct((len(places), TILE, CHUNK), BF16),
        compiler_params=params(),
        name=name,
    )(array)


def forward_tiles(place_ref, index_ref, panel_ref, *refs):
    tiles_refs, (mine_ref, other_ref, total) = refs[:X], refs[X:]
    core = place_ref[0]
    for step in range(X):
        block = place_ref[1] ^ step
        total[...] = jnp.zeros_like(total)
        for slot in range(SLOTS):
            row = index_ref[step, slot]
            col = index_ref[step, SLOTS + slot]
            valid = index_ref[step, 2 * SLOTS + slot]
            tile = tiles_refs[step][slot * TILE : (slot + 1) * TILE, :]
            product = jnp.dot(tile, panel_ref[col], preferred_element_type=F32)
            total[row] += jnp.where(valid > 0, product, 0.0)
        for pair in range(Z):
            mine_ref[block * Z + pair] = total[2 * pair + core].astype(BF16)
            other_ref[block * Z + pair] = total[2 * pair + 1 - core].astype(BF16)


def middle(core_ref, parts_ref, weight_ref, cotangent_ref, act_ref, grad_ref, keep_ref, send_ref):
    chunks = []
    for chunk in range(X):
        total = parts_ref[chunk * Z].astype(F32)
        for z in range(1, Z):
            total += parts_ref[chunk * Z + z].astype(F32)
        chunks.append(total)
    summed = jnp.concatenate(chunks, axis=1)
    high = summed.astype(BF16)
    low = (summed - high.astype(F32)).astype(BF16)
    weight = weight_ref[...]
    aggregated = jnp.dot(high, weight, preferred_element_type=F32) + jnp.dot(
        low, weight, preferred_element_type=F32
    )
    sig = jax.nn.sigmoid(aggregated)
    act_ref[...] = (aggregated * sig).astype(BF16)
    grad = (cotangent_ref[...].astype(F32) * sig * (1.0 + aggregated * (1.0 - sig))).astype(BF16)
    grad_ref[...] = grad
    weight_part = lax.dot_general(
        high, grad, (((0,), (0,)), ((), ())), preferred_element_type=F32
    ).astype(BF16)
    low_half, high_half = weight_part[: WIDTH // 2], weight_part[WIDTH // 2 :]
    upper = core_ref[0] == 1
    keep_ref[...] = jnp.where(upper, high_half, low_half)
    send_ref[...] = jnp.where(upper, low_half, high_half)


def backward_tiles(place_ref, index_ref, mine_ref, other_ref, *refs):
    tiles_refs, (out_ref, total) = refs[:X], refs[X:]
    core = place_ref[0]
    total[...] = jnp.zeros_like(total)
    for step in range(X):
        block = place_ref[1] ^ step
        for slot in range(SLOTS):
            row = index_ref[step, slot]
            col = index_ref[step, SLOTS + slot]
            valid = index_ref[step, 2 * SLOTS + slot]
            at = block * Z + row // 2
            panel = jnp.where(row % 2 == core, mine_ref[at], other_ref[at])
            tile = tiles_refs[step][slot * TILE : (slot + 1) * TILE, :]
            product = lax.dot_general(
                tile, panel, (((0,), (0,)), ((), ())), preferred_element_type=F32
            )
            total[col] += jnp.where(valid > 0, product, 0.0)
    for tile in range(COL_TILES):
        out_ref[tile] = total[tile].astype(BF16)


def last(parts_ref, weight_ref, out_ref):
    chunks = []
    for chunk in range(X):
        total = parts_ref[chunk].astype(F32)
        for y in range(1, Y):
            total += parts_ref[y * X + chunk].astype(F32)
        chunks.append(total)
    summed = jnp.concatenate(chunks, axis=1).astype(BF16)
    out_ref[...] = lax.dot_general(
        summed, weight_ref[...], (((1,), (1,)), ((), ())), preferred_element_type=F32
    ).astype(BF16)


def place_rows(place_ref, mine_ref, other_ref, out_ref):
    core = place_ref[0]
    half, share = WIDTH // CORES, WIDTH // (Y_LOW * CORES)
    scale = 1.0 / math.sqrt(TILE * Y * X * Z * CORES)
    for y in range(Y_LOW):
        for side, ref in ((core, mine_ref), (1 - core, other_ref)):
            start = pl.multiple_of(side * half + (y ^ place_ref[2]) * share, share)
            out_ref[pl.ds(start, share), :] = ref[y].astype(F32) * scale


def exchange(array, axis, distance):
    size = lax.axis_size(axis)
    return lax.ppermute(array, axis, [(i, i ^ distance) for i in range(size)])


def scatter(array, axis, flip):
    size, place = lax.axis_size(axis), lax.axis_index(axis) ^ flip
    shares = array.reshape(size, array.shape[0] // size, array.shape[1])

    def share(distance):
        return lax.dynamic_index_in_dim(shares, place ^ distance, 0, keepdims=False)

    total = share(0).astype(F32)
    for distance in range(1, size):
        total = total + exchange(share(distance), axis, distance).astype(F32)
    return total.astype(BF16)


def double(array, axis, distance):
    return (array.astype(F32) + exchange(array, axis, distance).astype(F32)).astype(BF16)


def double4(array, axis):
    one, two, three = (exchange(array, axis, distance).astype(F32) for distance in (1, 2, 3))
    return ((array.astype(F32) + one) + (two + three)).astype(BF16)


def body(features, weight, cotangent, tile_values, tile_rows, tile_cols, tile_valid):
    flip = lax.axis_index("y_high") * (Y_LOW - 1)
    place = jnp.stack([lax.axis_index("core"), lax.axis_index("x"), flip]).astype(jnp.int32)

    chunks = spread_chunks(features, [at % X for at in range(COL_TILES)], "spread_features")
    panel = lax.all_to_all(chunks, ROW, 0, 0, tiled=True)

    index = jnp.concatenate(
        [tile_rows.reshape(-1), tile_cols.reshape(-1), tile_valid.reshape(-1)]
    ).astype(BF16)
    index = jnp.pad(index[None, :], ((0, INDEX_ROWS - 1), (0, TILE - 3 * SLOTS)))
    tiles = jnp.concatenate([tile_values.reshape(SLOTS * TILE, TILE), index], axis=0)
    tiles = [tiles] + [exchange(tiles, "x", distance) for distance in range(1, X)]
    index = jnp.stack([t[SLOTS * TILE, : 3 * SLOTS] for t in tiles]).astype(jnp.int32)
    limit = jnp.repeat(jnp.array([ROW_TILES - 1, COL_TILES - 1, 1], jnp.int32), SLOTS)
    index = jnp.clip(index, 0, limit[None, :])

    mine, other = pl.pallas_call(
        forward_tiles,
        in_specs=[smem(), smem()] + [vmem()] * (1 + X),
        out_specs=[vmem()] * 2,
        out_shape=[jax.ShapeDtypeStruct((X * Z, TILE, CHUNK), BF16)] * 2,
        scratch_shapes=[pltpu.VMEM((ROW_TILES, TILE, CHUNK), F32)],
        compiler_params=params(),
        name="forward_tiles",
    )(place, index, panel, *tiles)
    term = (mine.astype(F32) + exchange(other, "core", 1).astype(F32)).astype(BF16)
    parts = lax.all_to_all(term, ("x", "z"), 0, 0, tiled=True)

    half = WIDTH // CORES
    activations, grad, weight_keep, weight_send = pl.pallas_call(
        middle,
        in_specs=[smem()] + [vmem()] * 3,
        out_specs=[vmem()] * 4,
        out_shape=[
            jax.ShapeDtypeStruct((TILE, WIDTH), BF16),
            jax.ShapeDtypeStruct((TILE, WIDTH), BF16),
            jax.ShapeDtypeStruct((half, WIDTH), BF16),
            jax.ShapeDtypeStruct((half, WIDTH), BF16),
        ],
        compiler_params=params(),
        name="middle",
    )(place, parts, weight, cotangent)

    grad = spread_chunks(grad, [at // Z for at in range(X * Z)], "spread_grad")
    piece = weight_keep.astype(F32) + exchange(weight_send, "core", 1).astype(F32)
    grad, piece = lax.optimization_barrier((grad, piece.astype(BF16)))
    grad_mine = lax.all_to_all(grad, ("x", "z"), 0, 0, tiled=True)
    piece = scatter(piece, "y_low", flip)
    piece = double(piece, ("y_high", "y_low"), Y - 1)
    piece = double(piece, "x", 1)
    grad_mine, piece = lax.optimization_barrier((grad_mine, piece))

    grad_other = exchange(grad_mine, "core", 1)
    back = pl.pallas_call(
        backward_tiles,
        in_specs=[smem(), smem()] + [vmem()] * (2 + X),
        out_specs=vmem(),
        out_shape=jax.ShapeDtypeStruct((COL_TILES, TILE, CHUNK), BF16),
        scratch_shapes=[pltpu.VMEM((COL_TILES, TILE, CHUNK), F32)],
        compiler_params=params(),
        name="backward_tiles",
    )(place, index, grad_mine, grad_other, *tiles)
    back, piece = lax.optimization_barrier((back, piece))
    back = lax.all_to_all(back, ROW, 0, 0, tiled=True)
    piece = double4(piece, "z")
    piece = double(piece, "z", Z - 1)
    piece = double(piece, "x", X - 1)
    back, piece = lax.optimization_barrier((back, piece))

    input_grad = pl.pallas_call(
        last,
        in_specs=[vmem()] * 2,
        out_specs=vmem(),
        out_shape=jax.ShapeDtypeStruct((TILE, WIDTH), BF16),
        compiler_params=params(),
        name="last",
    )(back, weight)

    share = WIDTH // (Y_LOW * CORES)
    piece = jnp.broadcast_to(piece[None], (Y_LOW, share, WIDTH))
    whole = lax.all_to_all(piece, "y_low", 0, 0, tiled=True)
    weight_grad = pl.pallas_call(
        place_rows,
        in_specs=[smem()] + [vmem()] * 2,
        out_specs=vmem(),
        out_shape=jax.ShapeDtypeStruct((WIDTH, WIDTH), F32),
        compiler_params=params(),
        name="place_rows",
    )(place, whole, exchange(whole, "core", 1))
    return (activations, input_grad, weight_grad)


def solution(mesh):
    axes = Mesh(mesh.devices.reshape(Y_HIGH, Y_LOW, X, Z, CORES), ROW + COL)
    placed = (
        P(COL + ROW, None),
        P(),
        P(ROW + COL, None),
        P(ROW, COL, None, None, None),
        P(ROW, COL, None),
        P(ROW, COL, None),
        P(ROW, COL, None),
    )
    return jax.shard_map(
        body,
        mesh=axes,
        in_specs=placed,
        out_specs=(P(ROW + COL, None), P(COL + ROW, None), P()),
        check_vma=False,
    )
```

```python
import functools
import math

import jax
import jax.numpy as jnp
from jax import lax
from jax.experimental import pallas as pl
from jax.experimental.pallas import tpu as pltpu
from jax.sharding import Mesh, PartitionSpec as P

Y_HIGH, Y_LOW, X, Z, CORES = 2, 4, 4, 8, 2
Y = Y_HIGH * Y_LOW
ROW = ("y_high", "y_low", "x")
COL = ("z", "core")
TILE = 128
SLOTS = 8
WIDTH = 512
CHUNK = WIDTH // X
ROW_TILES = Z * CORES
COL_TILES = Y * X
INDEX_ROWS = 16
BF16 = jnp.bfloat16
F32 = jnp.float32


def params():
    return pltpu.CompilerParams(vmem_limit_bytes=24 * 1024 * 1024)


def vmem():
    return pl.BlockSpec(memory_space=pltpu.VMEM)


def smem():
    return pl.BlockSpec(memory_space=pltpu.SMEM)


def spread(places, in_ref, out_ref, sems):
    copies = []
    for place, chunk in enumerate(places):
        piece = in_ref.at[:, pl.ds(chunk * CHUNK, CHUNK)]
        copies.append(pltpu.make_async_copy(piece, out_ref.at[place], sems.at[place]))
        copies[-1].start()
    for copy in copies:
        copy.wait()


def spread_chunks(array, places, name):
    return pl.pallas_call(
        functools.partial(spread, places),
        in_specs=[vmem()],
        out_specs=pl.BlockSpec(memory_space=pl.ANY),
        out_shape=jax.ShapeDtypeStruct((len(places), TILE, CHUNK), BF16),
        scratch_shapes=[pltpu.SemaphoreType.DMA((len(places),))],
        compiler_params=params(),
        name=name,
    )(array)


def forward_tiles(place_ref, index_ref, panel_ref, *refs):
    tiles_refs, (mine_ref, other_ref, total) = refs[:X], refs[X:]
    core = place_ref[0]
    for step in range(X):
        block = place_ref[1] ^ step
        total[...] = jnp.zeros_like(total)
        for slot in range(SLOTS):
            row = index_ref[step, slot]
            col = index_ref[step, SLOTS + slot]
            valid = index_ref[step, 2 * SLOTS + slot]
            tile = tiles_refs[step][slot * TILE : (slot + 1) * TILE, :]
            product = jnp.dot(tile, panel_ref[col], preferred_element_type=F32)
            total[row] += jnp.where(valid > 0, product, 0.0)
        for pair in range(Z):
            mine_ref[block * Z + pair] = total[2 * pair + core].astype(BF16)
            other_ref[block * Z + pair] = total[2 * pair + 1 - core].astype(BF16)


def middle(core_ref, parts_ref, weight_ref, cotangent_ref, act_ref, grad_ref, keep_ref, send_ref):
    chunks = []
    for chunk in range(X):
        total = parts_ref[chunk * Z].astype(F32)
        for z in range(1, Z):
            total += parts_ref[chunk * Z + z].astype(F32)
        chunks.append(total)
    summed = jnp.concatenate(chunks, axis=1)
    high = summed.astype(BF16)
    low = (summed - high.astype(F32)).astype(BF16)
    weight = weight_ref[...]
    aggregated = jnp.dot(high, weight, preferred_element_type=F32) + jnp.dot(
        low, weight, preferred_element_type=F32
    )
    sig = jax.nn.sigmoid(aggregated)
    act_ref[...] = (aggregated * sig).astype(BF16)
    grad = (cotangent_ref[...].astype(F32) * sig * (1.0 + aggregated * (1.0 - sig))).astype(BF16)
    grad_ref[...] = grad
    weight_part = lax.dot_general(
        high, grad, (((0,), (0,)), ((), ())), preferred_element_type=F32
    ).astype(BF16)
    low_half, high_half = weight_part[: WIDTH // 2], weight_part[WIDTH // 2 :]
    upper = core_ref[0] == 1
    keep_ref[...] = jnp.where(upper, high_half, low_half)
    send_ref[...] = jnp.where(upper, low_half, high_half)


def backward_tiles(place_ref, index_ref, mine_ref, other_ref, *refs):
    tiles_refs, (out_ref, total, done, sems) = refs[:X], refs[X:]
    core = place_ref[0]
    total[...] = jnp.zeros_like(total)
    for step in range(X):
        block = place_ref[1] ^ step
        for slot in range(SLOTS):
            row = index_ref[step, slot]
            col = index_ref[step, SLOTS + slot]
            valid = index_ref[step, 2 * SLOTS + slot]
            at = block * Z + row // 2
            panel = jnp.where(row % 2 == core, mine_ref[at], other_ref[at])
            tile = tiles_refs[step][slot * TILE : (slot + 1) * TILE, :]
            product = lax.dot_general(
                tile, panel, (((0,), (0,)), ((), ())), preferred_element_type=F32
            )
            total[col] += jnp.where(valid > 0, product, 0.0)
    copies = []
    for group in range(0, COL_TILES, X):
        done[group : group + X] = total[group : group + X].astype(BF16)
        here = pl.ds(group, X)
        copies.append(pltpu.make_async_copy(done.at[here], out_ref.at[here], sems.at[group // X]))
        copies[-1].start()
    for copy in copies:
        copy.wait()


def last(parts_ref, weight_ref, out_ref):
    chunks = []
    for chunk in range(X):
        total = parts_ref[chunk].astype(F32)
        for y in range(1, Y):
            total += parts_ref[y * X + chunk].astype(F32)
        chunks.append(total)
    summed = jnp.concatenate(chunks, axis=1).astype(BF16)
    out_ref[...] = lax.dot_general(
        summed, weight_ref[...], (((1,), (1,)), ((), ())), preferred_element_type=F32
    ).astype(BF16)


def place_rows(place_ref, mine_ref, other_ref, out_ref, held, sems):
    core = place_ref[0]
    half, share = WIDTH // CORES, WIDTH // (Y_LOW * CORES)
    scale = 1.0 / math.sqrt(TILE * Y * X * Z * CORES)
    copies = []
    for y in range(Y_LOW):
        for side, ref in ((core, mine_ref), (1 - core, other_ref)):
            start = pl.multiple_of(side * half + (y ^ place_ref[2]) * share, share)
            at = len(copies)
            held[at] = ref[y].astype(F32) * scale
            copies.append(pltpu.make_async_copy(held.at[at], out_ref.at[pl.ds(start, share), :], sems.at[at]))
            copies[-1].start()
    for copy in copies:
        copy.wait()


def exchange(array, axis, distance):
    size = lax.axis_size(axis)
    return lax.ppermute(array, axis, [(i, i ^ distance) for i in range(size)])


def scatter(array, axis, flip):
    size, place = lax.axis_size(axis), lax.axis_index(axis) ^ flip
    shares = array.reshape(size, array.shape[0] // size, array.shape[1])

    def share(distance):
        return lax.dynamic_index_in_dim(shares, place ^ distance, 0, keepdims=False)

    total = share(0).astype(F32)
    for distance in range(1, size):
        total = total + exchange(share(distance), axis, distance).astype(F32)
    return total.astype(BF16)


def double(array, axis, distance):
    return (array.astype(F32) + exchange(array, axis, distance).astype(F32)).astype(BF16)


def double4(array, axis):
    one, two, three = (exchange(array, axis, distance).astype(F32) for distance in (1, 2, 3))
    return ((array.astype(F32) + one) + (two + three)).astype(BF16)


def body(features, weight, cotangent, tile_values, tile_rows, tile_cols, tile_valid):
    flip = lax.axis_index("y_high") * (Y_LOW - 1)
    place = jnp.stack([lax.axis_index("core"), lax.axis_index("x"), flip]).astype(jnp.int32)

    chunks = spread_chunks(features, [at % X for at in range(COL_TILES)], "spread_features")
    panel = lax.all_to_all(chunks, ROW, 0, 0, tiled=True)

    index = jnp.concatenate(
        [tile_rows.reshape(-1), tile_cols.reshape(-1), tile_valid.reshape(-1)]
    ).astype(BF16)
    index = jnp.pad(index[None, :], ((0, INDEX_ROWS - 1), (0, TILE - 3 * SLOTS)))
    tiles = jnp.concatenate([tile_values.reshape(SLOTS * TILE, TILE), index], axis=0)
    tiles = [tiles] + [exchange(tiles, "x", distance) for distance in range(1, X)]
    index = jnp.stack([t[SLOTS * TILE, : 3 * SLOTS] for t in tiles]).astype(jnp.int32)
    limit = jnp.repeat(jnp.array([ROW_TILES - 1, COL_TILES - 1, 1], jnp.int32), SLOTS)
    index = jnp.clip(index, 0, limit[None, :])

    mine, other = pl.pallas_call(
        forward_tiles,
        in_specs=[smem(), smem()] + [vmem()] * (1 + X),
        out_specs=[vmem()] * 2,
        out_shape=[jax.ShapeDtypeStruct((X * Z, TILE, CHUNK), BF16)] * 2,
        scratch_shapes=[pltpu.VMEM((ROW_TILES, TILE, CHUNK), F32)],
        compiler_params=params(),
        name="forward_tiles",
    )(place, index, panel, *tiles)
    term = (mine.astype(F32) + exchange(other, "core", 1).astype(F32)).astype(BF16)
    parts = lax.all_to_all(term, ("x", "z"), 0, 0, tiled=True)

    half = WIDTH // CORES
    activations, grad, weight_keep, weight_send = pl.pallas_call(
        middle,
        in_specs=[smem()] + [vmem()] * 3,
        out_specs=[vmem()] * 4,
        out_shape=[
            jax.ShapeDtypeStruct((TILE, WIDTH), BF16),
            jax.ShapeDtypeStruct((TILE, WIDTH), BF16),
            jax.ShapeDtypeStruct((half, WIDTH), BF16),
            jax.ShapeDtypeStruct((half, WIDTH), BF16),
        ],
        compiler_params=params(),
        name="middle",
    )(place, parts, weight, cotangent)

    grad = spread_chunks(grad, [at // Z for at in range(X * Z)], "spread_grad")
    piece = weight_keep.astype(F32) + exchange(weight_send, "core", 1).astype(F32)
    grad, piece = lax.optimization_barrier((grad, piece.astype(BF16)))
    grad_mine = lax.all_to_all(grad, ("x", "z"), 0, 0, tiled=True)
    piece = scatter(piece, "y_low", flip)
    piece = double(piece, ("y_high", "y_low"), Y - 1)
    piece = double(piece, "x", 1)
    grad_mine, piece = lax.optimization_barrier((grad_mine, piece))

    grad_other = exchange(grad_mine, "core", 1)
    back = pl.pallas_call(
        backward_tiles,
        in_specs=[smem(), smem()] + [vmem()] * (2 + X),
        out_specs=pl.BlockSpec(memory_space=pl.ANY),
        out_shape=jax.ShapeDtypeStruct((COL_TILES, TILE, CHUNK), BF16),
        scratch_shapes=[
            pltpu.VMEM((COL_TILES, TILE, CHUNK), F32),
            pltpu.VMEM((COL_TILES, TILE, CHUNK), BF16),
            pltpu.SemaphoreType.DMA((Y,)),
        ],
        compiler_params=params(),
        name="backward_tiles",
    )(place, index, grad_mine, grad_other, *tiles)
    back, piece = lax.optimization_barrier((back, piece))
    back = lax.all_to_all(back, ROW, 0, 0, tiled=True)
    piece = double4(piece, "z")
    piece = double(piece, "z", Z - 1)
    piece = double(piece, "x", X - 1)
    back, piece = lax.optimization_barrier((back, piece))

    input_grad = pl.pallas_call(
        last,
        in_specs=[vmem()] * 2,
        out_specs=vmem(),
        out_shape=jax.ShapeDtypeStruct((TILE, WIDTH), BF16),
        compiler_params=params(),
        name="last",
    )(back, weight)

    share = WIDTH // (Y_LOW * CORES)
    piece = jnp.broadcast_to(piece[None], (Y_LOW, share, WIDTH))
    whole = lax.all_to_all(piece, "y_low", 0, 0, tiled=True)
    weight_grad = pl.pallas_call(
        place_rows,
        in_specs=[smem()] + [vmem()] * 2,
        out_specs=pl.BlockSpec(memory_space=pl.ANY),
        out_shape=jax.ShapeDtypeStruct((WIDTH, WIDTH), F32),
        scratch_shapes=[
            pltpu.VMEM((Y_LOW * CORES, share, WIDTH), F32),
            pltpu.SemaphoreType.DMA((Y_LOW * CORES,)),
        ],
        compiler_params=params(),
        name="place_rows",
    )(place, whole, exchange(whole, "core", 1))
    return (activations, input_grad, weight_grad)


def solution(mesh):
    axes = Mesh(mesh.devices.reshape(Y_HIGH, Y_LOW, X, Z, CORES), ROW + COL)
    placed = (
        P(COL + ROW, None),
        P(),
        P(ROW + COL, None),
        P(ROW, COL, None, None, None),
        P(ROW, COL, None),
        P(ROW, COL, None),
        P(ROW, COL, None),
    )
    return jax.shard_map(
        body,
        mesh=axes,
        in_specs=placed,
        out_specs=(P(ROW + COL, None), P(COL + ROW, None), P()),
        check_vma=False,
    )
```

```python
import functools
import math

import jax
import jax.numpy as jnp
from jax import lax
from jax.experimental import pallas as pl
from jax.experimental.pallas import tpu as pltpu
from jax.sharding import Mesh, PartitionSpec as P

Y_HIGH, Y_LOW, X, Z, CORES = 2, 4, 4, 8, 2
Y = Y_HIGH * Y_LOW
ROW = ("y_high", "y_low", "x")
COL = ("z", "core")
TILE = 128
SLOTS = 8
WIDTH = 512
CHUNK = WIDTH // X
ROW_TILES = Z * CORES
COL_TILES = Y * X
INDEX_ROWS = 16
BF16 = jnp.bfloat16
F32 = jnp.float32


def params():
    return pltpu.CompilerParams(vmem_limit_bytes=24 * 1024 * 1024)


def vmem():
    return pl.BlockSpec(memory_space=pltpu.VMEM)


def smem():
    return pl.BlockSpec(memory_space=pltpu.SMEM)


def spread(places, in_ref, out_ref):
    for place, chunk in enumerate(places):
        out_ref[place] = in_ref[:, chunk * CHUNK : (chunk + 1) * CHUNK]


def spread_chunks(array, places, name):
    return pl.pallas_call(
        functools.partial(spread, places),
        in_specs=[vmem()],
        out_specs=vmem(),
        out_shape=jax.ShapeDtypeStruct((len(places), TILE, CHUNK), BF16),
        compiler_params=params(),
        name=name,
    )(array)


def forward_tiles(place_ref, index_ref, panel_ref, *refs):
    tiles_refs, (mine_ref, other_ref, total) = refs[:X], refs[X:]
    core = place_ref[0]
    for step in range(X):
        block = place_ref[1] ^ step
        total[...] = jnp.zeros_like(total)
        for slot in range(SLOTS):
            row = index_ref[step, slot]
            col = index_ref[step, SLOTS + slot]
            valid = index_ref[step, 2 * SLOTS + slot]
            tile = tiles_refs[step][slot * TILE : (slot + 1) * TILE, :]
            product = jnp.dot(tile, panel_ref[col], preferred_element_type=F32)
            total[row] += jnp.where(valid > 0, product, 0.0)
        for pair in range(Z):
            mine_ref[block * Z + pair] = total[2 * pair + core].astype(BF16)
            other_ref[block * Z + pair] = total[2 * pair + 1 - core].astype(BF16)


def middle(core_ref, parts_ref, weight_ref, cotangent_ref, act_ref, grad_ref, keep_ref, send_ref):
    chunks = []
    for chunk in range(X):
        total = parts_ref[chunk * Z].astype(F32)
        for z in range(1, Z):
            total += parts_ref[chunk * Z + z].astype(F32)
        chunks.append(total)
    summed = jnp.concatenate(chunks, axis=1)
    high = summed.astype(BF16)
    low = (summed - high.astype(F32)).astype(BF16)
    weight = weight_ref[...]
    aggregated = jnp.dot(high, weight, preferred_element_type=F32) + jnp.dot(
        low, weight, preferred_element_type=F32
    )
    sig = jax.nn.sigmoid(aggregated)
    act_ref[...] = (aggregated * sig).astype(BF16)
    grad = (cotangent_ref[...].astype(F32) * sig * (1.0 + aggregated * (1.0 - sig))).astype(BF16)
    grad_ref[...] = grad
    weight_part = lax.dot_general(
        high, grad, (((0,), (0,)), ((), ())), preferred_element_type=F32
    ).astype(BF16)
    low_half, high_half = weight_part[: WIDTH // 2], weight_part[WIDTH // 2 :]
    upper = core_ref[0] == 1
    keep_ref[...] = jnp.where(upper, high_half, low_half)
    send_ref[...] = jnp.where(upper, low_half, high_half)


def backward_tiles(place_ref, index_ref, mine_ref, other_ref, *refs):
    tiles_refs, (out_ref, total) = refs[:X], refs[X:]
    core = place_ref[0]
    total[...] = jnp.zeros_like(total)
    for step in range(X):
        block = place_ref[1] ^ step
        for slot in range(SLOTS):
            row = index_ref[step, slot]
            col = index_ref[step, SLOTS + slot]
            valid = index_ref[step, 2 * SLOTS + slot]
            at = block * Z + row // 2
            panel = jnp.where(row % 2 == core, mine_ref[at], other_ref[at])
            tile = tiles_refs[step][slot * TILE : (slot + 1) * TILE, :]
            product = lax.dot_general(
                tile, panel, (((0,), (0,)), ((), ())), preferred_element_type=F32
            )
            total[col] += jnp.where(valid > 0, product, 0.0)
    for tile in range(COL_TILES):
        out_ref[tile] = total[tile].astype(BF16)


def last(parts_ref, weight_ref, out_ref):
    chunks = []
    for chunk in range(X):
        total = parts_ref[chunk].astype(F32)
        for y in range(1, Y):
            total += parts_ref[y * X + chunk].astype(F32)
        chunks.append(total)
    summed = jnp.concatenate(chunks, axis=1).astype(BF16)
    out_ref[...] = lax.dot_general(
        summed, weight_ref[...], (((1,), (1,)), ((), ())), preferred_element_type=F32
    ).astype(BF16)


def place_rows(place_ref, pieces_ref, out_ref):
    half, share = WIDTH // CORES, WIDTH // (Y_LOW * CORES)
    scale = 1.0 / math.sqrt(TILE * Y * X * Z * CORES)
    for y in range(Y_LOW):
        for core in range(CORES):
            start = pl.multiple_of(core * half + (y ^ place_ref[2]) * share, share)
            out_ref[pl.ds(start, share), :] = pieces_ref[y * CORES + core].astype(F32) * scale


def exchange(array, axis, distance):
    size = lax.axis_size(axis)
    return lax.ppermute(array, axis, [(i, i ^ distance) for i in range(size)])


def scatter(array, axis, flip):
    size, place = lax.axis_size(axis), lax.axis_index(axis) ^ flip
    shares = array.reshape(size, array.shape[0] // size, array.shape[1])

    def share(distance):
        return lax.dynamic_index_in_dim(shares, place ^ distance, 0, keepdims=False)

    total = share(0).astype(F32)
    for distance in range(1, size):
        total = total + exchange(share(distance), axis, distance).astype(F32)
    return total.astype(BF16)


def double(array, axis, distance):
    return (array.astype(F32) + exchange(array, axis, distance).astype(F32)).astype(BF16)


def double4(array, axis):
    one, two, three = (exchange(array, axis, distance).astype(F32) for distance in (1, 2, 3))
    return ((array.astype(F32) + one) + (two + three)).astype(BF16)


def body(features, weight, cotangent, tile_values, tile_rows, tile_cols, tile_valid):
    flip = lax.axis_index("y_high") * (Y_LOW - 1)
    place = jnp.stack([lax.axis_index("core"), lax.axis_index("x"), flip]).astype(jnp.int32)

    chunks = spread_chunks(features, [at % X for at in range(COL_TILES)], "spread_features")
    panel = lax.all_to_all(chunks, ROW, 0, 0, tiled=True)

    index = jnp.concatenate(
        [tile_rows.reshape(-1), tile_cols.reshape(-1), tile_valid.reshape(-1)]
    ).astype(BF16)
    index = jnp.pad(index[None, :], ((0, INDEX_ROWS - 1), (0, TILE - 3 * SLOTS)))
    tiles = jnp.concatenate([tile_values.reshape(SLOTS * TILE, TILE), index], axis=0)
    tiles = [tiles] + [exchange(tiles, "x", distance) for distance in range(1, X)]
    index = jnp.stack([t[SLOTS * TILE, : 3 * SLOTS] for t in tiles]).astype(jnp.int32)
    limit = jnp.repeat(jnp.array([ROW_TILES - 1, COL_TILES - 1, 1], jnp.int32), SLOTS)
    index = jnp.clip(index, 0, limit[None, :])

    mine, other = pl.pallas_call(
        forward_tiles,
        in_specs=[smem(), smem()] + [vmem()] * (1 + X),
        out_specs=[vmem()] * 2,
        out_shape=[jax.ShapeDtypeStruct((X * Z, TILE, CHUNK), BF16)] * 2,
        scratch_shapes=[pltpu.VMEM((ROW_TILES, TILE, CHUNK), F32)],
        compiler_params=params(),
        name="forward_tiles",
    )(place, index, panel, *tiles)
    term = (mine.astype(F32) + exchange(other, "core", 1).astype(F32)).astype(BF16)
    parts = lax.all_to_all(term, ("x", "z"), 0, 0, tiled=True)

    half = WIDTH // CORES
    activations, grad, weight_keep, weight_send = pl.pallas_call(
        middle,
        in_specs=[smem()] + [vmem()] * 3,
        out_specs=[vmem()] * 4,
        out_shape=[
            jax.ShapeDtypeStruct((TILE, WIDTH), BF16),
            jax.ShapeDtypeStruct((TILE, WIDTH), BF16),
            jax.ShapeDtypeStruct((half, WIDTH), BF16),
            jax.ShapeDtypeStruct((half, WIDTH), BF16),
        ],
        compiler_params=params(),
        name="middle",
    )(place, parts, weight, cotangent)

    grad = spread_chunks(grad, [at // Z for at in range(X * Z)], "spread_grad")
    piece = weight_keep.astype(F32) + exchange(weight_send, "core", 1).astype(F32)
    grad, piece = lax.optimization_barrier((grad, piece.astype(BF16)))
    grad_mine = lax.all_to_all(grad, ("x", "z"), 0, 0, tiled=True)
    piece = scatter(piece, "y_low", flip)
    piece = double(piece, ("y_high", "y_low"), Y - 1)
    piece = double(piece, "x", 1)
    grad_mine, piece = lax.optimization_barrier((grad_mine, piece))

    grad_other = exchange(grad_mine, "core", 1)
    back = pl.pallas_call(
        backward_tiles,
        in_specs=[smem(), smem()] + [vmem()] * (2 + X),
        out_specs=vmem(),
        out_shape=jax.ShapeDtypeStruct((COL_TILES, TILE, CHUNK), BF16),
        scratch_shapes=[pltpu.VMEM((COL_TILES, TILE, CHUNK), F32)],
        compiler_params=params(),
        name="backward_tiles",
    )(place, index, grad_mine, grad_other, *tiles)
    back, piece = lax.optimization_barrier((back, piece))
    back = lax.all_to_all(back, ROW, 0, 0, tiled=True)
    piece = double4(piece, "z")
    piece = double(piece, "z", Z - 1)
    piece = double(piece, "x", X - 1)
    back, piece = lax.optimization_barrier((back, piece))

    input_grad = pl.pallas_call(
        last,
        in_specs=[vmem()] * 2,
        out_specs=vmem(),
        out_shape=jax.ShapeDtypeStruct((TILE, WIDTH), BF16),
        compiler_params=params(),
        name="last",
    )(back, weight)

    share = WIDTH // (Y_LOW * CORES)
    piece = jnp.broadcast_to(piece[None], (Y_LOW * CORES, share, WIDTH))
    whole = lax.all_to_all(piece, ("y_low", "core"), 0, 0, tiled=True)
    weight_grad = pl.pallas_call(
        place_rows,
        in_specs=[smem(), vmem()],
        out_specs=vmem(),
        out_shape=jax.ShapeDtypeStruct((WIDTH, WIDTH), F32),
        compiler_params=params(),
        name="place_rows",
    )(place, whole)
    return (activations, input_grad, weight_grad)


def solution(mesh):
    axes = Mesh(mesh.devices.reshape(Y_HIGH, Y_LOW, X, Z, CORES), ROW + COL)
    placed = (
        P(COL + ROW, None),
        P(),
        P(ROW + COL, None),
        P(ROW, COL, None, None, None),
        P(ROW, COL, None),
        P(ROW, COL, None),
        P(ROW, COL, None),
    )
    return jax.shard_map(
        body,
        mesh=axes,
        in_specs=placed,
        out_specs=(P(ROW + COL, None), P(COL + ROW, None), P()),
        check_vma=False,
    )
```
